128 devices in a mesh: dp: 16 (over z, y), mp: 8 (over x, core).
Axes of the slice: x: 4, y: 4, z: 4, core: 2. Of those that a mesh axis runs over, the one named last changes fastest.
Arguments:
- hidden: bfloat16 [256, 5120], P('dp', 'mp'), may hold values from -6 to 6
- w_query: bfloat16 [5120, 8192], P(None, 'mp'), may hold values from -0.078125 to 0.078125
- w_key: bfloat16 [5120, 1024], P(None, 'mp'), may hold values from -0.078125 to 0.078125
- w_value: bfloat16 [5120, 1024], P(None, 'mp'), may hold values from -0.078125 to 0.078125
- query_gain: float32 [128], replicated, may hold values from 0.5 to 3
- key_gain: float32 [128], replicated, may hold values from 0.5 to 3
- kv_pool: bfloat16 [12288, 16, 8, 256], P('dp', None, 'mp')
- page_table: int32 [256, 48], replicated, may hold values from 0 to 767, as said below
- parent: int32 [256], replicated, may hold values from 0 to 255, as said below
- surviving: int32 [256], replicated, may hold values from 0 to 1, as said below
Outputs:
- refilled_pool: bfloat16 [12288, 16, 8, 256], P('dp', None, 'mp')
- attention: bfloat16 [256, 8192], P('dp', 'mp')
The draws below stay inside these ranges and needn't reach their ends.
Inputs may be any that keep to these rules, and one draw needn't show every extreme that they name: `page_table`: for each group, its 16 rows together name each page 0 to 767 once. A pruned branch's parent survives. For every group, at most 2 of its pruned branches have parents in any one group, and this is reached in every draw; those branches have different parents. For a surviving branch the entry names some surviving branch and is not used. `surviving`: each group keeps 2 to 4 of its branches.
All inputs are finite; a program needn't handle non-finite values.
Results may differ from the reference program's by a relative error of at most 0.015.
The reference program's roundings to bfloat16 on the way (of `query_rows`) count: a program that leaves them out, or rounds other values in their place, can miss the bound.
Values may be sent and summed in bfloat16 or wider, within the bound.
A program may use at most 128 MiB of HBM per device.

```python
import math
import jax
import jax.numpy as jnp
from jax import lax

D = 5120
H = 64
KVH = 8
HD = 128
PAGE = 16
NPAGE = 48
BR_DEV = 16
CAP = 2
BRANCHES = 256
POOL_DEV = 768
POOL = 12288


def routing(key):
    groups = BRANCHES // BR_DEV
    key_count, key_order, key_shift, key_pick, key_group, key_other = jax.random.split(key, 6)
    counts = jax.random.randint(key_count, (groups,), 2, 5)
    order_perm = jax.vmap(lambda subkey: jax.random.permutation(subkey, BR_DEV))(jax.random.split(key_order, groups))
    position = jnp.argsort(order_perm, axis=1)
    alive_mask = position < counts[:, None]
    child_mask = jnp.logical_not(alive_mask)
    child_rank = jnp.maximum(jnp.cumsum(child_mask.astype(jnp.int32), axis=1) - 1, 0)
    group_shift = jax.random.randint(key_shift, (groups,), 0, groups)
    group_ids = jnp.arange(groups, dtype=jnp.int32)
    src_group = (group_ids[:, None] + group_shift[:, None] + child_rank // CAP) % groups
    pair_base = jax.random.randint(key_pick, (groups, BR_DEV), 0, 12)
    base_pick = jnp.take_along_axis(pair_base, child_rank // CAP, axis=1)
    pick_index = (base_pick + child_rank % CAP) % counts[src_group]
    chosen = order_perm[src_group, pick_index]
    other_group = jax.random.randint(key_group, (groups, BR_DEV), 0, groups)
    other_pick = jax.random.randint(key_other, (groups, BR_DEV), 0, 12)
    other_chosen = order_perm[other_group, other_pick % counts[other_group]]
    parent_ids = jnp.where(alive_mask, other_group * BR_DEV + other_chosen, src_group * BR_DEV + chosen)
    return (alive_mask.reshape(-1).astype(jnp.int32), parent_ids.reshape(-1).astype(jnp.int32))


def draw_parent(key, part):
    return routing(key)[1]


def draw_surviving(key, part):
    return routing(key)[0]


def draw_page_table(key, part):
    key = jax.random.fold_in(key, 7)
    groups = BRANCHES // BR_DEV
    perms = jax.vmap(lambda subkey: jax.random.permutation(subkey, BR_DEV * NPAGE))(jax.random.split(key, groups))
    return perms.reshape(BRANCHES, NPAGE).astype(jnp.int32)


def draw_kv_pool(key, part):
    key = jax.random.fold_in(key, 11)
    key_first, key_second = jax.random.split(key, 2)
    shape = (POOL, PAGE, KVH, HD)
    keys_part = 2.5 * jax.random.normal(key_first, shape)
    values_part = jax.random.normal(key_second, shape)
    return jnp.concatenate([keys_part, values_part], axis=-1).astype(jnp.bfloat16)


def shard_levels(stream_key, extent, cuts, low, top_value):
    level, own = 1.0, jax.random.fold_in(stream_key, 6)
    for axis_at, blocks in cuts:
        draws = jnp.exp(jax.random.uniform(jax.random.fold_in(own, axis_at), (blocks,), jnp.float32, low / len(cuts), top_value / len(cuts)))
        level = level * jnp.repeat(draws, extent[axis_at] // blocks).reshape([-1 if axis == axis_at else 1 for axis in range(len(extent))])
    return level


def noise(key, shape, spread, reach, shards=(), held_as=jnp.bfloat16):
    level = shard_levels(key, shape, shards, -0.22, 0.18) if shards else 1.0
    array = jax.random.normal(key, shape, jnp.float32) * spread * level
    return jnp.minimum(jnp.maximum(array, -reach), reach).astype(held_as)


def setup_inputs(seed: int = 0) -> dict:
    keys = jax.random.split(jax.random.key(seed), 11)
    return {
        "hidden": noise(keys[0], (BRANCHES, D), 1.0, 6.0, ((0, 16), (1, 8))),
        "w_query": noise(keys[1], (D, H * HD), D ** -0.5, 0.078125, ((1, 8),)),
        "w_key": noise(keys[2], (D, KVH * HD), D ** -0.5, 0.078125, ((1, 8),)),
        "w_value": noise(keys[3], (D, KVH * HD), D ** -0.5, 0.078125, ((1, 8),)),
        "query_gain": jnp.clip(jnp.exp(jax.random.uniform(keys[4], (HD,), jnp.float32, math.log(0.5), math.log(3.0))), 0.5, 3.0),
        "key_gain": jnp.clip(jnp.exp(jax.random.uniform(keys[5], (HD,), jnp.float32, math.log(0.5), math.log(3.0))), 0.5, 3.0),
        "kv_pool": draw_kv_pool(jax.random.fold_in(keys[10], 71), 0),
        "page_table": draw_page_table(jax.random.fold_in(keys[10], 71), 0),
        "parent": draw_parent(jax.random.fold_in(keys[10], 71), 0),
        "surviving": draw_surviving(jax.random.fold_in(keys[10], 71), 0),
    }


def normalize(values, gain):
    return values * lax.rsqrt(lax.optimization_barrier(jnp.mean(values * values, -1, keepdims=True)) + 1e-06) * gain

def attend(query_one, key_one, value_one, window):
    keys_part = window[..., :HD].astype(jnp.float32)
    values_part = window[..., HD:].astype(jnp.float32)
    scores = jnp.einsum('kgd,tkd->kgt', query_one.astype(jnp.float32), keys_part)
    own_score = jnp.einsum('kgd,kd->kg', query_one.astype(jnp.float32), key_one.astype(jnp.float32))
    peak_score = jnp.maximum(lax.optimization_barrier(jnp.max(scores, -1)), own_score)
    expo_terms = jnp.exp(scores - peak_score[..., None])
    own_term = jnp.exp(own_score - peak_score)
    total_mass = lax.optimization_barrier(jnp.sum(expo_terms, -1)) + own_term
    weights = (expo_terms / total_mass[..., None]).astype(jnp.bfloat16)
    own_weight = (own_term / total_mass).astype(jnp.bfloat16)
    mixed_out = jnp.einsum('kgt,tkd->kgd', weights.astype(jnp.float32), values_part)
    mixed_out = mixed_out + own_weight.astype(jnp.float32)[..., None] * value_one.astype(jnp.float32)[:, None, :]
    return mixed_out.astype(jnp.bfloat16)

def reference(hidden, w_query, w_key, w_value, query_gain, key_gain, kv_pool, page_table, parent, surviving):
    head_group = H // KVH
    query_full = jnp.dot(hidden, w_query, preferred_element_type=jnp.float32).reshape(BRANCHES, KVH, head_group, HD)
    query_rows = (normalize(query_full, query_gain) / math.sqrt(HD)).astype(jnp.bfloat16)
    key_full = jnp.dot(hidden, w_key, preferred_element_type=jnp.float32).reshape(BRANCHES, KVH, HD)
    key_rows = normalize(key_full, key_gain).astype(jnp.bfloat16)
    value_rows = jnp.dot(hidden, w_value, preferred_element_type=jnp.float32).reshape(BRANCHES, KVH, HD).astype(jnp.bfloat16)
    slot_ids = jnp.arange(BRANCHES, dtype=jnp.int32)
    source = jnp.where(surviving > 0, slot_ids, parent).astype(jnp.int32)
    src_pages = (source // BR_DEV * POOL_DEV)[:, None] + page_table[source]
    dst_pages = (slot_ids // BR_DEV * POOL_DEV)[:, None] + page_table
    refilled = kv_pool.at[dst_pages.reshape(-1)].set(kv_pool[src_pages.reshape(-1)])

    def one_branch(inputs):
        query_one, key_one, value_one, pages_one = inputs
        window = refilled[pages_one].reshape(NPAGE * PAGE, KVH, 2 * HD)
        return attend(query_one, key_one, value_one, window)
    outputs = lax.map(one_branch, (query_rows, key_rows, value_rows, dst_pages))
    return (refilled, outputs.reshape(BRANCHES, H * HD))
```

```python
import math

import jax
import jax.numpy as jnp
from jax import lax
from jax.experimental import pallas as pl
from jax.experimental.pallas import tpu as pltpu
from jax.sharding import PartitionSpec as P

H = 64
KVH = 8
HD = 128
PAGE = 16
NPAGE = 48
BR = 16
GROUPS = 16
ALIVE = 4
KIDS = 14
SIDE = 4
NQ = 3
PQ = 2
PIECE = NQ * PQ
HALF = NPAGE // 2
MP = 8
MESH = pl.DeviceIdType.MESH
SLOTS = ALIVE + KIDS
CHUNK_TOKENS = SIDE * PQ * PAGE


def relay_kernel(
    hidden_ref, query_gain_ref, key_gain_ref, w_query_ref, w_key_ref, w_value_ref, pool_ref,
    table_ref, parent_ref, surviving_ref,
    arrived_out_ref, attention_ref,
    *scratch,
):
    scratch = list(scratch)
    gathered = [[scratch.pop(0) for _ in range(NQ)] for _ in range(2)]
    (outgoing, arrived, pool, features, w_query, w_key, w_value, project, queries, keys, values,
     peak, mass, mixed, result,
     alive_table, rank_table, source_table, child_table, slot_table,
     send_sem, recv_sem, feature_send, feature_recv, pool_sem, weight_sem, out_sem) = scratch

    group = lax.axis_index("dp")
    part = lax.axis_index("mp")
    z, y = group // SIDE, group % SIDE
    along = [z, y]
    across = [y, z]

    def device(half, gather_at, spread_at):
        if half == 0:
            return (gather_at * SIDE + spread_at, part)
        return (spread_at * SIDE + gather_at, part)

    def shifted(value, step, size=SIDE):
        return (value + step + size) % size

    pool_copy = pltpu.make_async_copy(pool_ref, pool, pool_sem)
    pool_copy.start()

    barrier = pltpu.get_barrier_semaphore()
    for step in range(1, SIDE):
        pl.semaphore_signal(barrier, inc=1, device_id=device(0, z, shifted(y, step)), device_id_type=MESH)
        pl.semaphore_signal(barrier, inc=1, device_id=device(1, y, shifted(z, step)), device_id_type=MESH)
    for step in range(1, MP):
        pl.semaphore_signal(barrier, inc=1, device_id=(group, shifted(part, step, MP)), device_id_type=MESH)

    def rank_group(at, carry):
        found = [jnp.int32(99) for _ in range(ALIVE)]
        count = jnp.int32(0)
        for branch in range(BR):
            lives = surviving_ref[at * BR + branch]
            rank_table[at * BR + branch] = count
            for k in range(ALIVE):
                found[k] = jnp.where((lives > 0) & (count == k), jnp.int32(branch), found[k])
            count = count + lives
        for k in range(ALIVE):
            alive_table[at * ALIVE + k] = found[k]
        return carry

    lax.fori_loop(0, GROUPS, rank_group, 0)

    def child_of(at_group, j):
        branch = j
        for k in range(ALIVE):
            branch = branch + jnp.where(alive_table[at_group * ALIVE + k] - k <= j, 1, 0)
        return jnp.minimum(branch, BR - 1)

    for half in range(2):
        for spread_at in range(SIDE):
            target = z * SIDE + spread_at if half == 0 else spread_at * SIDE + y

            def find_source(j, carry, half=half, spread_at=spread_at, target=target):
                parent = parent_ref[target * BR + child_of(target, j)]
                from_group = parent // BR
                rank = rank_table[parent]
                if half == 1:
                    from_group = (from_group % SIDE) * SIDE + from_group // SIDE
                source_table[(half * SIDE + spread_at) * KIDS + j] = from_group * ALIVE + rank
                return carry

            lax.fori_loop(0, KIDS, find_source, 0)

    def own_children(j, carry):
        child_table[j] = child_of(group, j)
        return carry

    lax.fori_loop(0, KIDS, own_children, 0)

    def own_slots(b, carry):
        rank = rank_table[group * BR + b]
        lives = surviving_ref[group * BR + b]
        slot_table[b] = jnp.minimum(jnp.where(lives > 0, rank, ALIVE + b - rank), SLOTS - 1)
        return carry

    lax.fori_loop(0, BR, own_slots, 0)
    pl.semaphore_wait(barrier, 2 * (SIDE - 1) + MP - 1)

    feature_copies = []
    for step in range(1, MP):
        copy = pltpu.make_async_remote_copy(
            src_ref=hidden_ref, dst_ref=features.at[part],
            send_sem=feature_send.at[step - 1], recv_sem=feature_recv.at[step - 1],
            device_id=(group, shifted(part, step, MP)), device_id_type=MESH)
        copy.start()
        feature_copies.append(copy)
    features[part] = hidden_ref[...]

    pool_copy.wait()
    weight_copies = []
    rows = hidden_ref.shape[1]
    for m in range(MP):
        some = pl.ds(m * rows, rows)
        copies = [
            pltpu.make_async_copy(source.at[some], target.at[some], weight_sem.at[m, i])
            for i, (source, target) in enumerate(
                ((w_query_ref, w_query), (w_key_ref, w_key), (w_value_ref, w_value)))
        ]
        for copy in copies:
            copy.start()
        weight_copies.append(copies)

    def remote(half, q, kind, source, target, gather_at, spread_at):
        return pltpu.make_async_remote_copy(
            src_ref=source, dst_ref=target,
            send_sem=send_sem.at[half, q, kind], recv_sem=recv_sem.at[half, q, kind],
            device_id=device(half, gather_at, spread_at), device_id_type=MESH)

    spread_copies, gather_copies, forward_copies, deliver_copies, out_copies = {}, {}, {}, {}, {}
    started = []

    for q in range(NQ):
        for half in range(2):
            def pack_alive(k, carry, q=q, half=half):
                branch = group * BR + jnp.minimum(alive_table[group * ALIVE + k], BR - 1)
                for spread_at in range(SIDE):
                    for r in range(PQ):
                        position = half * HALF + spread_at * PIECE + q * PQ + r
                        page = table_ref[position, branch]
                        arrived[half, q, spread_at, k, r] = pool[page]
                return carry

            lax.fori_loop(0, ALIVE, pack_alive, 0)
            a, c = along[half], across[half]
            here = pl.ds(a * 16 + c * 4, 4)
            copies = []
            for step in range(1, SIDE):
                to = shifted(c, step)
                copy = remote(
                    half, q, step - 1, arrived.at[half, q, to, pl.ds(0, ALIVE)], gathered[half][q].at[here], a, to)
                copy.start()
                copies.append(copy)
            gathered[half][q][here] = arrived[half, q, c, 0:ALIVE]
            spread_copies[half, q] = copies
            started += copies

    for q in range(NQ):
        for half in range(2):
            a, c = along[half], across[half]
            for copy in spread_copies[half, q]:
                copy.wait_recv()
            block = gathered[half][q].at[pl.ds(a * 16, 16)]
            copies = []
            for kind, step in ((3, 1), (4, -1)):
                copy = remote(half, q, kind, block, block, shifted(a, step), c)
                copy.start()
                copies.append(copy)
            gather_copies[half, q] = copies
            started += copies

    for copy in feature_copies:
        copy.wait_recv()
    project[...] = jnp.zeros_like(project)
    for m in range(MP):
        for copy in weight_copies[m]:
            copy.wait()
        some = pl.ds(m * rows, rows)
        part_rows = features[m]
        for i in range(4):
            columns = pl.ds(i * 256, 256)
            project[:, columns] += jnp.dot(
                part_rows, w_query[some, columns], preferred_element_type=jnp.float32)
        project[:, pl.ds(1024, HD)] += jnp.dot(part_rows, w_key[some], preferred_element_type=jnp.float32)
        project[:, pl.ds(1152, HD)] += jnp.dot(part_rows, w_value[some], preferred_element_type=jnp.float32)

    def normalize(block, gain):
        return block * lax.rsqrt(jnp.mean(block * block, -1, keepdims=True) + 1e-06) * gain

    for head in range(H // KVH):
        block = normalize(project[:, pl.ds(head * HD, HD)], query_gain_ref[...]) / math.sqrt(HD)
        queries[:, head, :] = block.astype(jnp.bfloat16).astype(jnp.float32)
    keys[:, 0, :] = normalize(project[:, pl.ds(1024, HD)], key_gain_ref[...]).astype(jnp.bfloat16).astype(jnp.float32)
    values[:, 0, :] = project[:, pl.ds(1152, HD)].astype(jnp.bfloat16).astype(jnp.float32)

    def slot_branch(slot):
        if slot < ALIVE:
            return jnp.minimum(alive_table[group * ALIVE + slot], BR - 1)
        return child_table[slot - ALIVE]

    branches = [slot_branch(slot) for slot in range(SLOTS)]
    for slot in range(SLOTS):
        branch = branches[slot]
        own_score = jnp.sum(queries[branch] * keys[branch], -1, keepdims=True)
        peak[slot] = jnp.broadcast_to(own_score, (H // KVH, HD))
        mass[slot] = jnp.ones((H // KVH, HD), jnp.float32)
        mixed[slot] = jnp.broadcast_to(values[branch], (H // KVH, HD))

    def attend(slot, window):
        tokens = window.reshape(CHUNK_TOKENS, 2 * HD)
        query = queries[branches[slot]].astype(jnp.bfloat16)
        scores = lax.dot_general(
            query, tokens[:, :HD], (((1,), (1,)), ((), ())), preferred_element_type=jnp.float32)
        old = peak[slot]
        new = jnp.maximum(old, jnp.max(scores, -1, keepdims=True))
        scale = jnp.exp(old - new)
        terms = jnp.exp(scores - new[:, :1])
        peak[slot] = new
        mass[slot] = mass[slot] * scale + jnp.sum(terms, -1, keepdims=True)
        mixed[slot] = mixed[slot] * scale + jnp.dot(
            terms.astype(jnp.bfloat16), tokens[:, HD:], preferred_element_type=jnp.float32)

    for q in range(NQ):
        for half in range(2):
            a, c = along[half], across[half]
            for copy in gather_copies[half, q]:
                copy.wait_recv()
            copies = []
            for kind, step, first in ((5, 1, 0), (6, -1, 8)):
                block = gathered[half][q].at[pl.ds(shifted(a, -step) * 16 + first, 8)]
                copy = remote(half, q, kind, block, block, shifted(a, step), c)
                copy.start()
                copies.append(copy)
            forward_copies[half, q] = copies
            started += copies

    for q in range(NQ):
        for half in range(2):
            for k in range(ALIVE):
                attend(k, arrived[half, q, :, k])

    for q in range(NQ):
        for half in range(2):
            a, c = along[half], across[half]
            for copy in forward_copies[half, q]:
                copy.wait_recv()
            for step in range(SIDE):
                to = shifted(c, step)

                def pack(j, carry, q=q, half=half, step=step, to=to):
                    source = source_table[(half * SIDE + to) * KIDS + j]
                    pages = gathered[half][q][source]
                    if step == 0:
                        arrived[half, q, to, ALIVE + j] = pages
                    else:
                        outgoing[half, q, step - 1, j] = pages
                    return carry

                lax.fori_loop(0, KIDS, pack, 0)
                if step:
                    copy = remote(
                        half, q, 6 + step, outgoing.at[half, q, step - 1],
                        arrived.at[half, q, c, pl.ds(ALIVE, KIDS)], a, to)
                    copy.start()
                    deliver_copies.setdefault((half, q), []).append(copy)
                    started.append(copy)

    for q in range(NQ):
        for half in range(2):
            for copy in deliver_copies[half, q]:
                copy.wait_recv()
            copy = pltpu.make_async_copy(arrived.at[half, q], arrived_out_ref.at[half, q], out_sem.at[half, q])
            copy.start()
            out_copies[half, q] = copy
            for j in range(KIDS):
                attend(ALIVE + j, arrived[half, q, :, ALIVE + j])

    for slot in range(SLOTS):
        mixed[slot] = mixed[slot] / mass[slot]
    for b in range(BR):
        result[b] = mixed[slot_table[b]]
    for head in range(H // KVH):
        attention_ref[:, pl.ds(head * HD, HD)] = result[:, head, :].astype(jnp.bfloat16)

    for copy in out_copies.values():
        copy.wait()
    for copy in started + feature_copies:
        copy.wait_send()


def refill_kernel(
    arrived_ref, table_ref, surviving_ref, refilled_ref, arrived, refilled, slot_table, in_sem, out_sem
):
    group = lax.axis_index("dp")
    loads = {}
    for q in range(NQ):
        for half in range(2):
            copy = pltpu.make_async_copy(arrived_ref.at[half, q], arrived.at[half, q], in_sem.at[half, q])
            copy.start()
            loads[half, q] = copy

    def find_slot(b, rank):
        lives = surviving_ref[group * BR + b] > 0
        slot_table[b] = jnp.minimum(jnp.where(lives, rank, ALIVE + b - rank), SLOTS - 1)
        return rank + jnp.where(lives, 1, 0)

    lax.fori_loop(0, BR, find_slot, jnp.int32(0))
    for (half, q), copy in loads.items():
        copy.wait()

        def place(b, carry, half=half, q=q):
            slot = slot_table[b]
            for c in range(SIDE):
                for r in range(PQ):
                    page = table_ref[half * HALF + c * PIECE + q * PQ + r, group * BR + b]
                    refilled[page] = arrived[half, q, c, slot, r]
            return carry

        lax.fori_loop(0, BR, place, 0)
    store = pltpu.make_async_copy(refilled, refilled_ref, out_sem)
    store.start()
    store.wait()


def shards(
    hidden, w_query, w_key, w_value, query_gain, key_gain, kv_pool, page_table, parent, surviving
):
    pool_pages = kv_pool.shape[0]
    pool = kv_pool.reshape(pool_pages, PAGE, 2 * HD)
    table = page_table.T
    vmem = pl.BlockSpec(memory_space=pltpu.VMEM)
    smem = pl.BlockSpec(memory_space=pltpu.SMEM)
    hbm = pl.BlockSpec(memory_space=pltpu.HBM)
    bf16, f32 = jnp.bfloat16, jnp.float32
    page_shape = (PAGE, 2 * HD)
    heads = H // KVH
    arrived, attention = pl.pallas_call(
        relay_kernel,
        out_shape=(
            jax.ShapeDtypeStruct((2, NQ, SIDE, SLOTS, PQ) + page_shape, bf16),
            jax.ShapeDtypeStruct((BR, heads * HD), bf16),
        ),
        in_specs=[vmem] * 3 + [hbm] * 4 + [smem] * 3,
        out_specs=(hbm, vmem),
        scratch_shapes=[pltpu.VMEM((GROUPS * ALIVE, PQ) + page_shape, bf16)] * (2 * NQ)
        + [
            pltpu.VMEM((2, NQ, SIDE - 1, KIDS, PQ) + page_shape, bf16),
            pltpu.VMEM((2, NQ, SIDE, SLOTS, PQ) + page_shape, bf16),
            pltpu.VMEM(pool.shape, bf16),
            pltpu.VMEM((MP,) + hidden.shape, bf16),
            pltpu.VMEM(w_query.shape, bf16),
            pltpu.VMEM(w_key.shape, bf16),
            pltpu.VMEM(w_value.shape, bf16),
            pltpu.VMEM((BR, heads * HD + 2 * HD), f32),
            pltpu.VMEM((BR, heads, HD), f32),
            pltpu.VMEM((BR, 1, HD), f32),
            pltpu.VMEM((BR, 1, HD), f32),
            pltpu.VMEM((SLOTS, heads, HD), f32),
            pltpu.VMEM((SLOTS, heads, HD), f32),
            pltpu.VMEM((SLOTS, heads, HD), f32),
            pltpu.VMEM((BR, heads, HD), f32),
            pltpu.SMEM((GROUPS * ALIVE,), jnp.int32),
            pltpu.SMEM((GROUPS * BR,), jnp.int32),
            pltpu.SMEM((2 * SIDE * KIDS,), jnp.int32),
            pltpu.SMEM((KIDS,), jnp.int32),
            pltpu.SMEM((BR,), jnp.int32),
            pltpu.SemaphoreType.DMA((2, NQ, 10)),
            pltpu.SemaphoreType.DMA((2, NQ, 10)),
            pltpu.SemaphoreType.DMA((MP - 1,)),
            pltpu.SemaphoreType.DMA((MP - 1,)),
            pltpu.SemaphoreType.DMA,
            pltpu.SemaphoreType.DMA((MP, 3)),
            pltpu.SemaphoreType.DMA((2, NQ)),
        ],
        compiler_params=pltpu.CompilerParams(
            collective_id=0, has_side_effects=True, vmem_limit_bytes=56 * 2**20),
        name="relay_pages_and_attend",
    )(
        hidden, query_gain.reshape(1, HD), key_gain.reshape(1, HD), w_query, w_key, w_value, pool,
        table, parent, surviving,
    )
    refilled = pl.pallas_call(
        refill_kernel,
        out_shape=jax.ShapeDtypeStruct(pool.shape, bf16),
        in_specs=[hbm, smem, smem],
        out_specs=hbm,
        scratch_shapes=[
            pltpu.VMEM(arrived.shape, bf16),
            pltpu.VMEM(pool.shape, bf16),
            pltpu.SMEM((BR,), jnp.int32),
            pltpu.SemaphoreType.DMA((2, NQ)),
            pltpu.SemaphoreType.DMA,
        ],
        compiler_params=pltpu.CompilerParams(vmem_limit_bytes=56 * 2**20),
        name="refill_pool",
    )(arrived, table, surviving)
    return (refilled.reshape(kv_pool.shape), attention)


def solution(mesh):
    return jax.shard_map(
        shards,
        mesh=mesh,
        in_specs=(
            P("dp", "mp"),
            P(None, "mp"),
            P(None, "mp"),
            P(None, "mp"),
            P(),
            P(),
            P("dp", None, "mp", None),
            P(),
            P(),
            P(),
        ),
        out_specs=(P("dp", None, "mp", None), P("dp", "mp")),
        check_vma=False,
    )
```

```python
import math

import jax
import jax.numpy as jnp
from jax import lax
from jax.experimental import pallas as pl
from jax.experimental.pallas import tpu as pltpu
from jax.sharding import PartitionSpec as P

H = 64
KVH = 8
HD = 128
PAGE = 16
NPAGE = 48
BR = 16
GROUPS = 16
ALIVE = 4
KIDS = 14
SIDE = 4
NQ = 3
PQ = 2
PIECE = NQ * PQ
HALF = NPAGE // 2
MP = 8
MESH = pl.DeviceIdType.MESH
SLOTS = ALIVE + KIDS
CHUNK_TOKENS = SIDE * PQ * PAGE
HEADS = H // KVH
RANGES = 6


def attend_chunk(arrived, queries, scores, terms, mixes, peak, mass, mixed, q, first, count):
    rows = pl.ds(first * HEADS, count * HEADS)
    windows = [
        [arrived[half, q, :, first + j].reshape(CHUNK_TOKENS, 2 * HD) for half in range(2)] for j in range(count)
    ]
    for j in range(count):
        query = queries[pl.ds((first + j) * HEADS, HEADS)].astype(jnp.bfloat16)
        for half in range(2):
            scores[pl.ds(j * HEADS, HEADS), pl.ds(half * CHUNK_TOKENS, CHUNK_TOKENS)] = lax.dot_general(
                query, windows[j][half][:, :HD], (((1,), (1,)), ((), ())), preferred_element_type=jnp.float32)
    part = pl.ds(0, count * HEADS)
    all_scores = scores[part]
    old = peak[rows]
    new = jnp.maximum(old, jnp.max(all_scores, -1, keepdims=True))
    scale = jnp.exp(old - new)
    all_terms = jnp.exp(all_scores - new[:, :1])
    terms[part] = all_terms
    for j in range(count):
        total = jnp.zeros((HEADS, HD), jnp.float32)
        for half in range(2):
            weights = terms[pl.ds(j * HEADS, HEADS), pl.ds(half * CHUNK_TOKENS, CHUNK_TOKENS)].astype(jnp.bfloat16)
            total += jnp.dot(weights, windows[j][half][:, HD:], preferred_element_type=jnp.float32)
        mixes[pl.ds(j * HEADS, HEADS)] = total
    new_mass = mass[rows] * scale + jnp.sum(all_terms, -1, keepdims=True)
    return new, new_mass, mixed[rows] * scale + mixes[part]


def relay_kernel(
    hidden_ref, query_gain_hbm, key_gain_hbm, w_query_ref, w_key_ref, w_value_ref, pool_ref,
    table_hbm, parent_hbm, surviving_hbm,
    arrived, slot_queries, peak, mass, mixed, places_ref,
    *scratch,
):
    scratch = list(scratch)
    gathered = [[scratch.pop(0) for _ in range(NQ)] for _ in range(2)]
    (outgoing, pool, features, w_query, w_key, w_value, project, queries, keys, values,
     scores, terms, mixes,
     query_gain_ref, key_gain_ref, table_ref, parent_ref, surviving_ref,
     alive_table, rank_table, source_table, child_table, slot_table,
     send_sem, recv_sem, feature_send, feature_recv, pool_sem, weight_sem, small_sem) = scratch

    group = lax.axis_index("dp")
    part = lax.axis_index("mp")
    z, y = group // SIDE, group % SIDE
    along = [z, y]
    across = [y, z]

    def device(half, gather_at, spread_at):
        if half == 0:
            return (gather_at * SIDE + spread_at, part)
        return (spread_at * SIDE + gather_at, part)

    def shifted(value, step, size=SIDE):
        return (value + step + size) % size

    pool_copy = pltpu.make_async_copy(pool_ref, pool, pool_sem)
    small_copies = [
        pltpu.make_async_copy(source, target, small_sem.at[i])
        for i, (source, target) in enumerate((
            (surviving_hbm, surviving_ref), (parent_hbm, parent_ref), (table_hbm, table_ref),
            (query_gain_hbm, query_gain_ref), (key_gain_hbm, key_gain_ref),
            (hidden_ref, features.at[part])))
    ]
    for copy in small_copies:
        copy.start()
    pool_copy.start()

    barrier = pltpu.get_barrier_semaphore()
    for step in range(1, SIDE):
        pl.semaphore_signal(barrier, inc=1, device_id=device(0, z, shifted(y, step)), device_id_type=MESH)
        pl.semaphore_signal(barrier, inc=1, device_id=device(1, y, shifted(z, step)), device_id_type=MESH)
    for step in range(1, MP):
        pl.semaphore_signal(barrier, inc=1, device_id=(group, shifted(part, step, MP)), device_id_type=MESH)

    def rank_group(at, carry):
        found = [jnp.int32(99) for _ in range(ALIVE)]
        count = jnp.int32(0)
        for branch in range(BR):
            lives = surviving_ref[at * BR + branch]
            rank_table[at * BR + branch] = count
            for k in range(ALIVE):
                found[k] = jnp.where((lives > 0) & (count == k), jnp.int32(branch), found[k])
            count = count + lives
        for k in range(ALIVE):
            alive_table[at * ALIVE + k] = found[k]
        return carry

    def child_of(at_group, j):
        branch = j
        for k in range(ALIVE):
            branch = branch + jnp.where(alive_table[at_group * ALIVE + k] - k <= j, 1, 0)
        return jnp.minimum(branch, BR - 1)

    def find_sources():
        for half in range(2):
            for spread_at in range(SIDE):
                target = z * SIDE + spread_at if half == 0 else spread_at * SIDE + y

                def find_source(j, carry, half=half, spread_at=spread_at, target=target):
                    parent = parent_ref[target * BR + child_of(target, j)]
                    from_group = parent // BR
                    rank = rank_table[parent]
                    if half == 1:
                        from_group = (from_group % SIDE) * SIDE + from_group // SIDE
                    source_table[(half * SIDE + spread_at) * KIDS + j] = from_group * ALIVE + rank
                    return carry

                lax.fori_loop(0, KIDS, find_source, 0)

        def own_children(j, carry):
            child_table[j] = child_of(group, j)
            return carry

        lax.fori_loop(0, KIDS, own_children, 0)

        def own_slots(b, carry):
            rank = rank_table[group * BR + b]
            lives = surviving_ref[group * BR + b]
            slot_table[b] = jnp.minimum(jnp.where(lives > 0, rank, ALIVE + b - rank), SLOTS - 1)
            return carry

        lax.fori_loop(0, BR, own_slots, 0)

    def invert_table():
        row = lax.broadcasted_iota(jnp.int32, (8, 128), 0)
        lane = lax.broadcasted_iota(jnp.int32, (8, 128), 1)
        page_ids = row * 128 + lane

        def one_branch(b, places):
            slot = slot_table[b]
            places = jnp.where((row == 7) & (lane == b), slot, places)
            for half in range(2):
                for c in range(SIDE):
                    for q in range(NQ):
                        for r in range(PQ):
                            page = table_ref[half * HALF + c * PIECE + q * PQ + r, group * BR + b]
                            place = (((half * NQ + q) * SIDE + c) * SLOTS + slot) * PQ + r
                            places = jnp.where(page_ids == page, place, places)
            return places

        places_ref[...] = lax.fori_loop(0, BR, one_branch, jnp.zeros((8, 128), jnp.int32))

    feature_copies, weight_copies = [], []
    rows = hidden_ref.shape[1]

    def send_features():
        for step in range(1, MP):
            copy = pltpu.make_async_remote_copy(
                src_ref=hidden_ref, dst_ref=features.at[part],
                send_sem=feature_send.at[step - 1], recv_sem=feature_recv.at[step - 1],
                device_id=(group, shifted(part, step, MP)), device_id_type=MESH)
            copy.start()
            feature_copies.append(copy)

    def load_weights():
        for m in range(MP):
            some = pl.ds(m * rows, rows)
            copies = [
                pltpu.make_async_copy(source.at[some], target.at[some], weight_sem.at[m, i])
                for i, (source, target) in enumerate(
                    ((w_query_ref, w_query), (w_key_ref, w_key), (w_value_ref, w_value)))
            ]
            for copy in copies:
                copy.start()
            weight_copies.append(copies)

    def remote(half, q, kind, source, target, gather_at, spread_at):
        return pltpu.make_async_remote_copy(
            src_ref=source, dst_ref=target,
            send_sem=send_sem.at[half, q, kind], recv_sem=recv_sem.at[half, q, kind],
            device_id=device(half, gather_at, spread_at), device_id_type=MESH)

    spread_copies, gather_copies, forward_copies, deliver_copies = {}, {}, {}, {}
    started = []

    def pack_alive(q):
        def one(k, carry):
            branch = group * BR + jnp.minimum(alive_table[group * ALIVE + k], BR - 1)
            for half in range(2):
                for spread_at in range(SIDE):
                    for r in range(PQ):
                        page = table_ref[half * HALF + spread_at * PIECE + q * PQ + r, branch]
                        arrived[half, q, spread_at, k, r] = pool[page]
            return carry

        lax.fori_loop(0, ALIVE, one, 0)

    def spread(q):
        for half in range(2):
            a, c = along[half], across[half]
            here = pl.ds(a * 16 + c * 4, 4)
            copies = []
            for step in (1, 3, 2):
                to = shifted(c, step)
                copy = remote(
                    half, q, step - 1, arrived.at[half, q, to, pl.ds(0, ALIVE)], gathered[half][q].at[here], a, to)
                copy.start()
                copies.append(copy)
            gathered[half][q][here] = arrived[half, q, c, 0:ALIVE]
            spread_copies[half, q] = copies
            started.extend(copies)

    def gather(q):
        for half in range(2):
            a, c = along[half], across[half]
            for copy in spread_copies[half, q]:
                copy.wait_recv()
            block = gathered[half][q].at[pl.ds(a * 16, 16)]
            copies = []
            for kind, step in ((3, 1), (4, -1)):
                copy = remote(half, q, kind, block, block, shifted(a, step), c)
                copy.start()
                copies.append(copy)
            gather_copies[half, q] = copies
            started.extend(copies)

    def forward(q):
        for half in range(2):
            a, c = along[half], across[half]
            for copy in gather_copies[half, q]:
                copy.wait_recv()
            copies = []
            for kind, step, first in ((5, 1, 0), (6, -1, 8)):
                block = gathered[half][q].at[pl.ds(shifted(a, -step) * 16 + first, 8)]
                copy = remote(half, q, kind, block, block, shifted(a, step), c)
                copy.start()
                copies.append(copy)
            forward_copies[half, q] = copies
            started.extend(copies)

    def deliver(q):
        for half in range(2):
            a, c = along[half], across[half]
            for copy in forward_copies[half, q]:
                copy.wait_recv()
            deliver_copies[half, q] = []
            for step in (1, 3, 2, 0):
                to = shifted(c, step)

                def pack(j, carry, half=half, step=step, to=to):
                    pages = gathered[half][q][source_table[(half * SIDE + to) * KIDS + j]]
                    if step == 0:
                        arrived[half, q, to, ALIVE + j] = pages
                    else:
                        outgoing[half, q, step - 1, j] = pages
                    return carry

                lax.fori_loop(0, KIDS, pack, 0)
                if step:
                    copy = remote(
                        half, q, 6 + step, outgoing.at[half, q, step - 1],
                        arrived.at[half, q, c, pl.ds(ALIVE, KIDS)], a, to)
                    copy.start()
                    deliver_copies[half, q].append(copy)
                    started.append(copy)

    def normalize(block, gain):
        return block * lax.rsqrt(jnp.mean(block * block, -1, keepdims=True) + 1e-06) * gain

    def project_tokens():
        for copy in small_copies[3:]:
            copy.wait()
        for copy in feature_copies:
            copy.wait_recv()
        project[...] = jnp.zeros_like(project)
        for m in range(MP):
            for copy in weight_copies[m]:
                copy.wait()
            some = pl.ds(m * rows, rows)
            part_rows = features[m]
            for i in range(4):
                columns = pl.ds(i * 256, 256)
                project[:, columns] += jnp.dot(
                    part_rows, w_query[some, columns], preferred_element_type=jnp.float32)
            project[:, pl.ds(1024, HD)] += jnp.dot(part_rows, w_key[some], preferred_element_type=jnp.float32)
            project[:, pl.ds(1152, HD)] += jnp.dot(part_rows, w_value[some], preferred_element_type=jnp.float32)
        for head in range(HEADS):
            block = normalize(project[:, pl.ds(head * HD, HD)], query_gain_ref[...]) / math.sqrt(HD)
            queries[:, head, :] = block.astype(jnp.bfloat16).astype(jnp.float32)
        key_rows = normalize(project[:, pl.ds(1024, HD)], key_gain_ref[...])
        keys[:, 0, :] = key_rows.astype(jnp.bfloat16).astype(jnp.float32)
        values[:, 0, :] = project[:, pl.ds(1152, HD)].astype(jnp.bfloat16).astype(jnp.float32)

    def start_attention():
        for slot in range(SLOTS):
            if slot < ALIVE:
                branch = jnp.minimum(alive_table[group * ALIVE + slot], BR - 1)
            else:
                branch = child_table[slot - ALIVE]
            some = pl.ds(slot * HEADS, HEADS)
            query = queries[branch]
            slot_queries[some] = query
            own_score = jnp.sum(query * keys[branch], -1, keepdims=True)
            peak[some] = jnp.broadcast_to(own_score, (HEADS, HD))
            mass[some] = jnp.ones((HEADS, HD), jnp.float32)
            mixed[some] = jnp.broadcast_to(values[branch], (HEADS, HD))

    def attend(q, first, count):
        some = pl.ds(first * HEADS, count * HEADS)
        peak[some], mass[some], mixed[some] = attend_chunk(
            arrived, slot_queries, scores, terms, mixes, peak, mass, mixed, q, first, count)

    small_copies[0].wait()
    lax.fori_loop(0, GROUPS, rank_group, 0)
    small_copies[1].wait()
    find_sources()
    small_copies[2].wait()
    pool_copy.wait()
    pack_alive(0)
    pl.semaphore_wait(barrier, 2 * (SIDE - 1) + MP - 1)
    spread(0)
    for q in range(1, NQ):
        pack_alive(q)
        spread(q)
    send_features()
    load_weights()
    for q in range(NQ):
        gather(q)
    invert_table()
    for q in range(NQ):
        forward(q)
    for q in range(NQ):
        deliver(q)
    project_tokens()
    start_attention()
    for q in range(NQ):
        attend(q, 0, ALIVE)
    for q in range(NQ):
        for half in range(2):
            for copy in deliver_copies[half, q]:
                copy.wait_recv()
        if q < NQ - 1:
            attend(q, ALIVE, KIDS)
    for copy in started + feature_copies:
        copy.wait_send()


def refill_kernel(
    arrived, slot_queries, peak, mass, mixed, places_ref,
    refilled_ref, attention_ref,
    refilled, scores, terms, mixes, final, result, store_sem,
):
    pages = arrived.reshape(2 * NQ * SIDE * SLOTS * PQ, PAGE, 2 * HD)
    stores = []
    for part in range(RANGES):
        def place(i, carry, part=part):
            refilled[part * 128 + i] = pages[places_ref[part, i]]
            return carry

        lax.fori_loop(0, 128, place, 0, unroll=8)
        some = pl.ds(part * 128, 128)
        copy = pltpu.make_async_copy(refilled.at[some], refilled_ref.at[some], store_sem.at[part])
        copy.start()
        stores.append(copy)
    alive = pl.ds(0, ALIVE * HEADS)
    final[alive] = mixed[alive] / mass[alive]
    _, total, mix = attend_chunk(
        arrived, slot_queries, scores, terms, mixes, peak, mass, mixed, NQ - 1, ALIVE, KIDS)
    final[pl.ds(ALIVE * HEADS, KIDS * HEADS)] = mix / total
    for b in range(BR):
        result[b] = final[pl.ds(pl.multiple_of(places_ref[7, b] * HEADS, HEADS), HEADS)]
    for head in range(HEADS):
        attention_ref[:, pl.ds(head * HD, HD)] = result[:, head, :].astype(jnp.bfloat16)
    for copy in stores:
        copy.wait()


def shards(
    hidden, w_query, w_key, w_value, query_gain, key_gain, kv_pool, page_table, parent, surviving
):
    pool_pages = kv_pool.shape[0]
    pool = kv_pool.reshape(pool_pages, PAGE, 2 * HD)
    table = page_table.T
    vmem = pl.BlockSpec(memory_space=pltpu.VMEM)
    smem = pl.BlockSpec(memory_space=pltpu.SMEM)
    hbm = pl.BlockSpec(memory_space=pltpu.HBM)
    bf16, f32, i32 = jnp.bfloat16, jnp.float32, jnp.int32
    page_shape = (PAGE, 2 * HD)
    state = pltpu.VMEM((SLOTS * HEADS, HD), f32)
    chunk = [
        pltpu.VMEM((KIDS * HEADS, 2 * CHUNK_TOKENS), f32),
        pltpu.VMEM((KIDS * HEADS, 2 * CHUNK_TOKENS), f32),
        pltpu.VMEM((KIDS * HEADS, HD), f32),
    ]
    operands = [
        pltpu.with_memory_space_constraint(x, pltpu.HBM)
        for x in (hidden, query_gain.reshape(1, HD), key_gain.reshape(1, HD), w_query, w_key, w_value, pool,
                  table, parent, surviving)
    ]
    *kept, places = pl.pallas_call(
        relay_kernel,
        out_shape=(
            pltpu.VMEM((2, NQ, SIDE, SLOTS, PQ) + page_shape, bf16),
            state, state, state, state,
            jax.ShapeDtypeStruct((8, 128), i32),
        ),
        in_specs=[hbm] * 10,
        out_specs=(vmem,) * 6,
        scratch_shapes=[pltpu.VMEM((GROUPS * ALIVE, PQ) + page_shape, bf16)] * (2 * NQ)
        + [
            pltpu.VMEM((2, NQ, SIDE - 1, KIDS, PQ) + page_shape, bf16),
            pltpu.VMEM(pool.shape, bf16),
            pltpu.VMEM((MP,) + hidden.shape, bf16),
            pltpu.VMEM(w_query.shape, bf16),
            pltpu.VMEM(w_key.shape, bf16),
            pltpu.VMEM(w_value.shape, bf16),
            pltpu.VMEM((BR, HEADS * HD + 2 * HD), f32),
            pltpu.VMEM((BR, HEADS, HD), f32),
            pltpu.VMEM((BR, 1, HD), f32),
            pltpu.VMEM((BR, 1, HD), f32),
            *chunk,
            pltpu.VMEM((1, HD), f32),
            pltpu.VMEM((1, HD), f32),
            pltpu.SMEM(table.shape, i32),
            pltpu.SMEM(parent.shape, i32),
            pltpu.SMEM(surviving.shape, i32),
            pltpu.SMEM((GROUPS * ALIVE,), i32),
            pltpu.SMEM((GROUPS * BR,), i32),
            pltpu.SMEM((2 * SIDE * KIDS,), i32),
            pltpu.SMEM((KIDS,), i32),
            pltpu.SMEM((BR,), i32),
            pltpu.SemaphoreType.DMA((2, NQ, 10)),
            pltpu.SemaphoreType.DMA((2, NQ, 10)),
            pltpu.SemaphoreType.DMA((MP - 1,)),
            pltpu.SemaphoreType.DMA((MP - 1,)),
            pltpu.SemaphoreType.DMA,
            pltpu.SemaphoreType.DMA((MP, 3)),
            pltpu.SemaphoreType.DMA((6,)),
        ],
        compiler_params=pltpu.CompilerParams(
            collective_id=0, has_side_effects=True, vmem_limit_bytes=44 * 2**20),
        name="relay_pages_and_attend",
    )(*operands)
    refilled, attention = pl.pallas_call(
        refill_kernel,
        out_shape=(
            jax.ShapeDtypeStruct(pool.shape, bf16),
            jax.ShapeDtypeStruct((BR, HEADS * HD), bf16),
        ),
        in_specs=[vmem] * 5 + [smem],
        out_specs=(hbm, vmem),
        scratch_shapes=[
            pltpu.VMEM(pool.shape, bf16),
            *chunk,
            pltpu.VMEM((SLOTS * HEADS, HD), f32),
            pltpu.VMEM((BR, HEADS, HD), f32),
            pltpu.SemaphoreType.DMA((RANGES,)),
        ],
        compiler_params=pltpu.CompilerParams(vmem_limit_bytes=44 * 2**20),
        name="refill_pool",
    )(*kept, places)
    return (refilled.reshape(kv_pool.shape), attention)


def solution(mesh):
    return jax.shard_map(
        shards,
        mesh=mesh,
        in_specs=(
            P("dp", "mp"),
            P(None, "mp"),
            P(None, "mp"),
            P(None, "mp"),
            P(),
            P(),
            P("dp", None, "mp", None),
            P(),
            P(),
            P(),
        ),
        out_specs=(P("dp", None, "mp", None), P("dp", "mp")),
        check_vma=False,
    )
```

```python
import math

import jax
import jax.numpy as jnp
from jax import lax
from jax.experimental import pallas as pl
from jax.experimental.pallas import tpu as pltpu
from jax.sharding import PartitionSpec as P

H = 64
KVH = 8
HD = 128
PAGE = 16
NPAGE = 48
BR = 16
GROUPS = 16
ALIVE = 4
KIDS = 14
SIDE = 4
NQ = 3
PQ = 2
PIECE = NQ * PQ
HALF = NPAGE // 2
MP = 8
MESH = pl.DeviceIdType.MESH
SLOTS = ALIVE + KIDS
CHUNK_TOKENS = SIDE * PQ * PAGE
HEADS = H // KVH
RANGES = 12
BATCH = 7


def attend_chunk(arrived, queries, scores, terms, mixes, peak, mass, mixed, q, first, count):
    rows = pl.ds(first * HEADS, count * HEADS)
    windows = [
        jnp.concatenate(
            [arrived[half, q, :, first + j].reshape(CHUNK_TOKENS, 2 * HD) for half in range(2)], axis=0)
        for j in range(count)
    ]
    for j in range(count):
        query = queries[pl.ds((first + j) * HEADS, HEADS)].astype(jnp.bfloat16)
        scores[pl.ds(j * HEADS, HEADS)] = lax.dot_general(
            query, windows[j][:, :HD], (((1,), (1,)), ((), ())), preferred_element_type=jnp.float32)
    part = pl.ds(0, count * HEADS)
    all_scores = scores[part]
    old = peak[rows]
    new = jnp.maximum(old, jnp.max(all_scores, -1, keepdims=True))
    scale = jnp.exp(old - new)
    all_terms = jnp.exp(all_scores - new[:, :1])
    terms[part] = all_terms
    for j in range(count):
        weights = terms[pl.ds(j * HEADS, HEADS)].astype(jnp.bfloat16)
        mixes[pl.ds(j * HEADS, HEADS)] = jnp.dot(
            weights, windows[j][:, HD:], preferred_element_type=jnp.float32)
    new_mass = mass[rows] * scale + jnp.sum(all_terms, -1, keepdims=True)
    return new, new_mass, mixed[rows] * scale + mixes[part]


def relay_kernel(
    hidden_ref, query_gain_hbm, key_gain_hbm, w_query_ref, w_key_ref, w_value_ref, pool_ref,
    table_hbm, parent_hbm, surviving_hbm,
    arrived, slot_queries, peak, mass, mixed, places_ref,
    *scratch,
):
    scratch = list(scratch)
    gathered = [[scratch.pop(0) for _ in range(NQ)] for _ in range(2)]
    (outgoing, pool, features, w_query, w_key, w_value, project, queries, keys, values,
     scores, terms, mixes,
     query_gain_ref, key_gain_ref, table_ref, parent_ref, surviving_ref,
     alive_table, rank_table, source_table, child_table, slot_table,
     send_sem, recv_sem, feature_send, feature_recv, pool_sem, weight_sem, small_sem) = scratch

    group = lax.axis_index("dp")
    part = lax.axis_index("mp")
    z, y = group // SIDE, group % SIDE
    along = [z, y]
    across = [y, z]

    def device(half, gather_at, spread_at):
        if half == 0:
            return (gather_at * SIDE + spread_at, part)
        return (spread_at * SIDE + gather_at, part)

    def shifted(value, step, size=SIDE):
        return (value + step + size) % size

    pool_copies = [
        pltpu.make_async_copy(pool_ref.at[pl.ds(i * 64, 64)], pool.at[pl.ds(i * 64, 64)], pool_sem.at[i])
        for i in range(RANGES)
    ]
    small_copies = [
        pltpu.make_async_copy(source, target, small_sem.at[i])
        for i, (source, target) in enumerate((
            (surviving_hbm, surviving_ref), (parent_hbm, parent_ref), (table_hbm, table_ref),
            (query_gain_hbm, query_gain_ref), (key_gain_hbm, key_gain_ref),
            (hidden_ref, features.at[part])))
    ]
    for copy in small_copies:
        copy.start()
    for copy in pool_copies:
        copy.start()

    barrier = pltpu.get_barrier_semaphore()
    for step in range(1, SIDE):
        pl.semaphore_signal(barrier, inc=1, device_id=device(0, z, shifted(y, step)), device_id_type=MESH)
        pl.semaphore_signal(barrier, inc=1, device_id=device(1, y, shifted(z, step)), device_id_type=MESH)
    for step in range(1, MP):
        pl.semaphore_signal(barrier, inc=1, device_id=(group, shifted(part, step, MP)), device_id_type=MESH)

    def rank_group(at, carry):
        found = [jnp.int32(99) for _ in range(ALIVE)]
        count = jnp.int32(0)
        for branch in range(BR):
            lives = surviving_ref[at * BR + branch]
            rank_table[at * BR + branch] = count
            for k in range(ALIVE):
                found[k] = jnp.where((lives > 0) & (count == k), jnp.int32(branch), found[k])
            count = count + lives
        for k in range(ALIVE):
            alive_table[at * ALIVE + k] = found[k]
        return carry

    def child_of(at_group, j):
        branch = j
        for k in range(ALIVE):
            branch = branch + jnp.where(alive_table[at_group * ALIVE + k] - k <= j, 1, 0)
        return jnp.minimum(branch, BR - 1)

    def find_sources():
        for half in range(2):
            for spread_at in range(SIDE):
                target = z * SIDE + spread_at if half == 0 else spread_at * SIDE + y

                def find_source(j, carry, half=half, spread_at=spread_at, target=target):
                    parent = parent_ref[target * BR + child_of(target, j)]
                    from_group = parent // BR
                    rank = rank_table[parent]
                    if half == 1:
                        from_group = (from_group % SIDE) * SIDE + from_group // SIDE
                    source_table[(half * SIDE + spread_at) * KIDS + j] = from_group * ALIVE + rank
                    return carry

                lax.fori_loop(0, KIDS, find_source, 0)

        def own_children(j, carry):
            child_table[j] = child_of(group, j)
            return carry

        lax.fori_loop(0, KIDS, own_children, 0)

        def own_slots(b, carry):
            rank = rank_table[group * BR + b]
            lives = surviving_ref[group * BR + b]
            slot_table[b] = jnp.minimum(jnp.where(lives > 0, rank, ALIVE + b - rank), SLOTS - 1)
            return carry

        lax.fori_loop(0, BR, own_slots, 0)

    def invert_table():
        row = lax.broadcasted_iota(jnp.int32, (8, 128), 0)
        lane = lax.broadcasted_iota(jnp.int32, (8, 128), 1)
        page_ids = row * 128 + lane

        def one_branch(b, places):
            slot = slot_table[b]
            places = jnp.where((row == 7) & (lane == b), slot, places)
            for half in range(2):
                for c in range(SIDE):
                    for q in range(NQ):
                        for r in range(PQ):
                            page = table_ref[half * HALF + c * PIECE + q * PQ + r, group * BR + b]
                            place = (((half * NQ + q) * SIDE + c) * SLOTS + slot) * PQ + r
                            places = jnp.where(page_ids == page, place, places)
            return places

        places_ref[...] = lax.fori_loop(0, BR, one_branch, jnp.zeros((8, 128), jnp.int32))

    feature_copies, weight_copies = [], []
    rows = hidden_ref.shape[1]

    def send_features():
        for step in range(1, MP):
            copy = pltpu.make_async_remote_copy(
                src_ref=hidden_ref, dst_ref=features.at[part],
                send_sem=feature_send.at[step - 1], recv_sem=feature_recv.at[step - 1],
                device_id=(group, shifted(part, step, MP)), device_id_type=MESH)
            copy.start()
            feature_copies.append(copy)

    def load_weights():
        for m in range(MP):
            some = pl.ds(m * rows, rows)
            copies = [
                pltpu.make_async_copy(source.at[some], target.at[some], weight_sem.at[m, i])
                for i, (source, target) in enumerate(
                    ((w_query_ref, w_query), (w_key_ref, w_key), (w_value_ref, w_value)))
            ]
            for copy in copies:
                copy.start()
            weight_copies.append(copies)

    def remote(half, q, kind, source, target, gather_at, spread_at):
        return pltpu.make_async_remote_copy(
            src_ref=source, dst_ref=target,
            send_sem=send_sem.at[half, q, kind], recv_sem=recv_sem.at[half, q, kind],
            device_id=device(half, gather_at, spread_at), device_id_type=MESH)

    spread_copies, gather_copies, forward_copies, deliver_copies = {}, {}, {}, {}
    started = []

    def pack_alive(q):
        def one(k, carry):
            branch = group * BR + jnp.minimum(alive_table[group * ALIVE + k], BR - 1)
            for half in range(2):
                where = [(spread_at, r) for spread_at in range(SIDE) for r in range(PQ)]
                pages = [table_ref[half * HALF + spread_at * PIECE + q * PQ + r, branch] for spread_at, r in where]
                blocks = [pool[page] for page in pages]
                for (spread_at, r), block in zip(where, blocks):
                    arrived[half, q, spread_at, k, r] = block
            return carry

        lax.fori_loop(0, ALIVE, one, 0)

    def spread(q):
        for half in range(2):
            a, c = along[half], across[half]
            here = pl.ds(a * 16 + c * 4, 4)
            copies = []
            for step in (2, 1, 3):
                to = shifted(c, step)
                copy = remote(
                    half, q, step - 1, arrived.at[half, q, to, pl.ds(0, ALIVE)], gathered[half][q].at[here], a, to)
                copy.start()
                copies.append(copy)
            gathered[half][q][here] = arrived[half, q, c, 0:ALIVE]
            spread_copies[half, q] = copies
            started.extend(copies)

    def gather(q):
        for half in range(2):
            a, c = along[half], across[half]
            for copy in spread_copies[half, q]:
                copy.wait_recv()
            block = gathered[half][q].at[pl.ds(a * 16, 16)]
            copies = []
            for kind, step in ((3, 1), (4, -1)):
                copy = remote(half, q, kind, block, block, shifted(a, step), c)
                copy.start()
                copies.append(copy)
            gather_copies[half, q] = copies
            started.extend(copies)

    def forward(q):
        for half in range(2):
            a, c = along[half], across[half]
            for copy in gather_copies[half, q]:
                copy.wait_recv()
            copies = []
            for kind, step, first in ((5, 1, 0), (6, -1, 8)):
                block = gathered[half][q].at[pl.ds(shifted(a, -step) * 16 + first, 8)]
                copy = remote(half, q, kind, block, block, shifted(a, step), c)
                copy.start()
                copies.append(copy)
            forward_copies[half, q] = copies
            started.extend(copies)

    def deliver(q):
        for half in range(2):
            a, c = along[half], across[half]
            for copy in forward_copies[half, q]:
                copy.wait_recv()
            deliver_copies[half, q] = []
            for step in (2, 1, 3, 0):
                to = shifted(c, step)

                def pack(batch, carry, half=half, step=step, to=to):
                    slots = [batch * BATCH + i for i in range(BATCH)]
                    sources = [source_table[(half * SIDE + to) * KIDS + j] for j in slots]
                    blocks = [gathered[half][q][source] for source in sources]
                    for j, block in zip(slots, blocks):
                        if step == 0:
                            arrived[half, q, to, ALIVE + j] = block
                        else:
                            outgoing[half, q, step - 1, j] = block
                    return carry

                lax.fori_loop(0, KIDS // BATCH, pack, 0)
                if step:
                    copy = remote(
                        half, q, 6 + step, outgoing.at[half, q, step - 1],
                        arrived.at[half, q, c, pl.ds(ALIVE, KIDS)], a, to)
                    copy.start()
                    deliver_copies[half, q].append(copy)
                    started.append(copy)

    def normalize(block, gain):
        return block * lax.rsqrt(jnp.mean(block * block, -1, keepdims=True) + 1e-06) * gain

    def project_tokens():
        for copy in small_copies[3:]:
            copy.wait()
        for copy in feature_copies:
            copy.wait_recv()
        project[...] = jnp.zeros_like(project)
        for m in range(MP):
            for copy in weight_copies[m]:
                copy.wait()
            some = pl.ds(m * rows, rows)
            part_rows = features[m]
            for i in range(4):
                columns = pl.ds(i * 256, 256)
                project[:, columns] += jnp.dot(
                    part_rows, w_query[some, columns], preferred_element_type=jnp.float32)
            project[:, pl.ds(1024, HD)] += jnp.dot(part_rows, w_key[some], preferred_element_type=jnp.float32)
            project[:, pl.ds(1152, HD)] += jnp.dot(part_rows, w_value[some], preferred_element_type=jnp.float32)
        for head in range(HEADS):
            block = normalize(project[:, pl.ds(head * HD, HD)], query_gain_ref[...]) / math.sqrt(HD)
            queries[:, head, :] = block.astype(jnp.bfloat16).astype(jnp.float32)
        key_rows = normalize(project[:, pl.ds(1024, HD)], key_gain_ref[...])
        keys[:, 0, :] = key_rows.astype(jnp.bfloat16).astype(jnp.float32)
        values[:, 0, :] = project[:, pl.ds(1152, HD)].astype(jnp.bfloat16).astype(jnp.float32)

    def start_attention():
        for slot in range(SLOTS):
            if slot < ALIVE:
                branch = jnp.minimum(alive_table[group * ALIVE + slot], BR - 1)
            else:
                branch = child_table[slot - ALIVE]
            some = pl.ds(slot * HEADS, HEADS)
            query = queries[branch]
            slot_queries[some] = query
            own_score = jnp.sum(query * keys[branch], -1, keepdims=True)
            peak[some] = jnp.broadcast_to(own_score, (HEADS, HD))
            mass[some] = jnp.ones((HEADS, HD), jnp.float32)
            mixed[some] = jnp.broadcast_to(values[branch], (HEADS, HD))

    def attend(q, first, count):
        some = pl.ds(first * HEADS, count * HEADS)
        peak[some], mass[some], mixed[some] = attend_chunk(
            arrived, slot_queries, scores, terms, mixes, peak, mass, mixed, q, first, count)

    small_copies[0].wait()
    rank_group(group, 0)
    small_copies[2].wait()
    for copy in pool_copies:
        copy.wait()
    pack_alive(0)
    pl.semaphore_wait(barrier, 2 * (SIDE - 1) + MP - 1)
    spread(0)
    for q in range(1, NQ):
        pack_alive(q)
        spread(q)
    send_features()
    load_weights()
    small_copies[1].wait()
    lax.fori_loop(0, GROUPS, rank_group, 0)
    find_sources()
    for q in range(NQ):
        gather(q)
    invert_table()
    for q in range(NQ):
        forward(q)
    for q in range(NQ):
        deliver(q)
    project_tokens()
    start_attention()
    for q in range(NQ):
        attend(q, 0, ALIVE)
    late = [copy for half in range(2) for copy in deliver_copies[half, NQ - 1]]
    for q in range(NQ - 1):
        for half in range(2):
            for copy in deliver_copies[half, q]:
                copy.wait_recv()
        attend(q, ALIVE, KIDS)
    for copy in started + feature_copies:
        if all(copy is not other for other in late):
            copy.wait_send()
    for copy in late:
        copy.wait()


def refill_kernel(
    arrived, slot_queries, peak, mass, mixed, places_ref,
    refilled_ref, attention_ref,
    refilled, scores, terms, mixes, final, result, store_sem,
):
    pages = arrived.reshape(2 * NQ * SIDE * SLOTS * PQ, PAGE, 2 * HD)
    stores = []
    for part in range(RANGES):
        def place(batch, carry, part=part):
            at = [batch * 8 + i for i in range(8)]
            places = [places_ref[part // 2, part % 2 * 64 + i] for i in at]
            blocks = [pages[place] for place in places]
            for i, block in zip(at, blocks):
                refilled[part * 64 + i] = block
            return carry

        lax.fori_loop(0, 8, place, 0)
        some = pl.ds(part * 64, 64)
        copy = pltpu.make_async_copy(refilled.at[some], refilled_ref.at[some], store_sem.at[part])
        copy.start()
        stores.append(copy)
    alive = pl.ds(0, ALIVE * HEADS)
    final[alive] = mixed[alive] / mass[alive]
    _, total, mix = attend_chunk(
        arrived, slot_queries, scores, terms, mixes, peak, mass, mixed, NQ - 1, ALIVE, KIDS)
    final[pl.ds(ALIVE * HEADS, KIDS * HEADS)] = mix / total
    for b in range(BR):
        result[b] = final[pl.ds(pl.multiple_of(places_ref[7, b] * HEADS, HEADS), HEADS)]
    for head in range(HEADS):
        attention_ref[:, pl.ds(head * HD, HD)] = result[:, head, :].astype(jnp.bfloat16)
    for copy in stores:
        copy.wait()


def shards(
    hidden, w_query, w_key, w_value, query_gain, key_gain, kv_pool, page_table, parent, surviving
):
    pool_pages = kv_pool.shape[0]
    pool = kv_pool.reshape(pool_pages, PAGE, 2 * HD)
    table = page_table.T
    vmem = pl.BlockSpec(memory_space=pltpu.VMEM)
    smem = pl.BlockSpec(memory_space=pltpu.SMEM)
    hbm = pl.BlockSpec(memory_space=pltpu.HBM)
    bf16, f32, i32 = jnp.bfloat16, jnp.float32, jnp.int32
    page_shape = (PAGE, 2 * HD)
    state = pltpu.VMEM((SLOTS * HEADS, HD), f32)
    chunk = [
        pltpu.VMEM((KIDS * HEADS, 2 * CHUNK_TOKENS), f32),
        pltpu.VMEM((KIDS * HEADS, 2 * CHUNK_TOKENS), f32),
        pltpu.VMEM((KIDS * HEADS, HD), f32),
    ]
    operands = [
        pltpu.with_memory_space_constraint(x, pltpu.HBM)
        for x in (hidden, query_gain.reshape(1, HD), key_gain.reshape(1, HD), w_query, w_key, w_value, pool,
                  table, parent, surviving)
    ]
    *kept, places = pl.pallas_call(
        relay_kernel,
        out_shape=(
            pltpu.VMEM((2, NQ, SIDE, SLOTS, PQ) + page_shape, bf16),
            state, state, state, state,
            jax.ShapeDtypeStruct((8, 128), i32),
        ),
        in_specs=[hbm] * 10,
        out_specs=(vmem,) * 6,
        scratch_shapes=[pltpu.VMEM((GROUPS * ALIVE, PQ) + page_shape, bf16)] * (2 * NQ)
        + [
            pltpu.VMEM((2, NQ, SIDE - 1, KIDS, PQ) + page_shape, bf16),
            pltpu.VMEM(pool.shape, bf16),
            pltpu.VMEM((MP,) + hidden.shape, bf16),
            pltpu.VMEM(w_query.shape, bf16),
            pltpu.VMEM(w_key.shape, bf16),
            pltpu.VMEM(w_value.shape, bf16),
            pltpu.VMEM((BR, HEADS * HD + 2 * HD), f32),
            pltpu.VMEM((BR, HEADS, HD), f32),
            pltpu.VMEM((BR, 1, HD), f32),
            pltpu.VMEM((BR, 1, HD), f32),
            *chunk,
            pltpu.VMEM((1, HD), f32),
            pltpu.VMEM((1, HD), f32),
            pltpu.SMEM(table.shape, i32),
            pltpu.SMEM(parent.shape, i32),
            pltpu.SMEM(surviving.shape, i32),
            pltpu.SMEM((GROUPS * ALIVE,), i32),
            pltpu.SMEM((GROUPS * BR,), i32),
            pltpu.SMEM((2 * SIDE * KIDS,), i32),
            pltpu.SMEM((KIDS,), i32),
            pltpu.SMEM((BR,), i32),
            pltpu.SemaphoreType.DMA((2, NQ, 10)),
            pltpu.SemaphoreType.DMA((2, NQ, 10)),
            pltpu.SemaphoreType.DMA((MP - 1,)),
            pltpu.SemaphoreType.DMA((MP - 1,)),
            pltpu.SemaphoreType.DMA((RANGES,)),
            pltpu.SemaphoreType.DMA((MP, 3)),
            pltpu.SemaphoreType.DMA((6,)),
        ],
        compiler_params=pltpu.CompilerParams(
            collective_id=0, has_side_effects=True, vmem_limit_bytes=44 * 2**20),
        name="relay_pages_and_attend",
    )(*operands)
    refilled, attention = pl.pallas_call(
        refill_kernel,
        out_shape=(
            jax.ShapeDtypeStruct(pool.shape, bf16),
            jax.ShapeDtypeStruct((BR, HEADS * HD), bf16),
        ),
        in_specs=[vmem] * 5 + [smem],
        out_specs=(hbm, vmem),
        scratch_shapes=[
            pltpu.VMEM(pool.shape, bf16),
            *chunk,
            pltpu.VMEM((SLOTS * HEADS, HD), f32),
            pltpu.VMEM((BR, HEADS, HD), f32),
            pltpu.SemaphoreType.DMA((RANGES,)),
        ],
        compiler_params=pltpu.CompilerParams(vmem_limit_bytes=44 * 2**20),
        name="refill_pool",
    )(*kept, places)
    return (refilled.reshape(kv_pool.shape), attention)


def solution(mesh):
    return jax.shard_map(
        shards,
        mesh=mesh,
        in_specs=(
            P("dp", "mp"),
            P(None, "mp"),
            P(None, "mp"),
            P(None, "mp"),
            P(),
            P(),
            P("dp", None, "mp", None),
            P(),
            P(),
            P(),
        ),
        out_specs=(P("dp", None, "mp", None), P("dp", "mp")),
        check_vma=False,
    )
```

```python
import math

import jax
import jax.numpy as jnp
from jax import lax
from jax.experimental import pallas as pl
from jax.experimental.pallas import tpu as pltpu
from jax.sharding import PartitionSpec as P

H = 64
KVH = 8
HD = 128
PAGE = 16
NPAGE = 48
BR = 16
GROUPS = 16
ALIVE = 4
KIDS = 14
SIDE = 4
NQ = 3
PQ = 2
PIECE = NQ * PQ
HALF = NPAGE // 2
MP = 8
MESH = pl.DeviceIdType.MESH
SLOTS = ALIVE + KIDS
CHUNK_TOKENS = SIDE * PQ * PAGE
HEADS = H // KVH
RANGES = 12
BATCH = 7


def attend_chunk(arrived, queries, scores, terms, mixes, peak, mass, mixed, q, first, count):
    rows = pl.ds(first * HEADS, count * HEADS)
    windows = [
        jnp.concatenate(
            [arrived[half, q, :, first + j].reshape(CHUNK_TOKENS, 2 * HD) for half in range(2)], axis=0)
        for j in range(count)
    ]
    for j in range(count):
        query = queries[pl.ds((first + j) * HEADS, HEADS)].astype(jnp.bfloat16)
        scores[pl.ds(j * HEADS, HEADS)] = lax.dot_general(
            query, windows[j][:, :HD], (((1,), (1,)), ((), ())), preferred_element_type=jnp.float32)
    part = pl.ds(0, count * HEADS)
    all_scores = scores[part]
    old = peak[rows]
    new = jnp.maximum(old, jnp.max(all_scores, -1, keepdims=True))
    scale = jnp.exp(old - new)
    all_terms = jnp.exp(all_scores - new[:, :1])
    terms[part] = all_terms
    for j in range(count):
        weights = terms[pl.ds(j * HEADS, HEADS)].astype(jnp.bfloat16)
        mixes[pl.ds(j * HEADS, HEADS)] = jnp.dot(
            weights, windows[j][:, HD:], preferred_element_type=jnp.float32)
    new_mass = mass[rows] * scale + jnp.sum(all_terms, -1, keepdims=True)
    return new, new_mass, mixed[rows] * scale + mixes[part]


def relay_kernel(
    hidden_ref, query_gain_hbm, key_gain_hbm, w_query_ref, w_key_ref, w_value_ref, pool_ref,
    table_hbm, parent_hbm, surviving_hbm,
    arrived, slot_queries, peak, mass, mixed, places_ref,
    *scratch,
):
    scratch = list(scratch)
    gathered = [[scratch.pop(0) for _ in range(NQ)] for _ in range(2)]
    (outgoing, pool, features, w_query, w_key, w_value, project, queries, keys, values,
     scores, terms, mixes, places,
     query_gain_ref, key_gain_ref, table_ref, parent_ref, surviving_ref,
     alive_table, rank_table, source_table, child_table, slot_table,
     send_sem, recv_sem, feature_send, feature_recv, pool_sem, weight_sem, small_sem, places_sem) = scratch

    group = lax.axis_index("dp")
    part = lax.axis_index("mp")
    z, y = group // SIDE, group % SIDE
    along = [z, y]
    across = [y, z]

    def device(half, gather_at, spread_at):
        if half == 0:
            return (gather_at * SIDE + spread_at, part)
        return (spread_at * SIDE + gather_at, part)

    def shifted(value, step, size=SIDE):
        return (value + step + size) % size

    pool_copies = [
        pltpu.make_async_copy(pool_ref.at[pl.ds(i * 64, 64)], pool.at[pl.ds(i * 64, 64)], pool_sem.at[i])
        for i in range(RANGES)
    ]
    barrier = pltpu.get_barrier_semaphore()
    for step in range(1, SIDE):
        pl.semaphore_signal(barrier, inc=1, device_id=device(0, z, shifted(y, step)), device_id_type=MESH)
        pl.semaphore_signal(barrier, inc=1, device_id=device(1, y, shifted(z, step)), device_id_type=MESH)
    for step in range(1, MP):
        pl.semaphore_signal(barrier, inc=1, device_id=(group, shifted(part, step, MP)), device_id_type=MESH)

    small_copies = [
        pltpu.make_async_copy(source, target, small_sem.at[i])
        for i, (source, target) in enumerate((
            (surviving_hbm, surviving_ref), (parent_hbm, parent_ref), (table_hbm, table_ref),
            (query_gain_hbm, query_gain_ref), (key_gain_hbm, key_gain_ref),
            (hidden_ref, features.at[part])))
    ]
    for copy in small_copies:
        copy.start()
    for copy in pool_copies:
        copy.start()

    def rank_group(at, carry):
        found = [jnp.int32(99) for _ in range(ALIVE)]
        count = jnp.int32(0)
        for branch in range(BR):
            lives = surviving_ref[at * BR + branch]
            rank_table[at * BR + branch] = count
            for k in range(ALIVE):
                found[k] = jnp.where((lives > 0) & (count == k), jnp.int32(branch), found[k])
            count = count + lives
        for k in range(ALIVE):
            alive_table[at * ALIVE + k] = found[k]
        return carry

    def child_of(at_group, j):
        branch = j
        for k in range(ALIVE):
            branch = branch + jnp.where(alive_table[at_group * ALIVE + k] - k <= j, 1, 0)
        return jnp.minimum(branch, BR - 1)

    def find_sources():
        for half in range(2):
            for spread_at in range(SIDE):
                target = z * SIDE + spread_at if half == 0 else spread_at * SIDE + y

                def find_source(j, carry, half=half, spread_at=spread_at, target=target):
                    parent = parent_ref[target * BR + child_of(target, j)]
                    from_group = parent // BR
                    rank = rank_table[parent]
                    if half == 1:
                        from_group = (from_group % SIDE) * SIDE + from_group // SIDE
                    source_table[(half * SIDE + spread_at) * KIDS + j] = from_group * ALIVE + rank
                    return carry

                lax.fori_loop(0, KIDS, find_source, 0)

        def own_children(j, carry):
            child_table[j] = child_of(group, j)
            return carry

        lax.fori_loop(0, KIDS, own_children, 0)

        def own_slots(b, carry):
            rank = rank_table[group * BR + b]
            lives = surviving_ref[group * BR + b]
            slot_table[b] = jnp.minimum(jnp.where(lives > 0, rank, ALIVE + b - rank), SLOTS - 1)
            return carry

        lax.fori_loop(0, BR, own_slots, 0)

    def invert_table():
        row = lax.broadcasted_iota(jnp.int32, (8, 128), 0)
        lane = lax.broadcasted_iota(jnp.int32, (8, 128), 1)
        page_ids = row * 128 + lane

        def one_branch(b, found):
            slot = slot_table[b]
            found = jnp.where((row == 7) & (lane == b), slot, found)
            for half in range(2):
                for c in range(SIDE):
                    for q in range(NQ):
                        for r in range(PQ):
                            page = table_ref[half * HALF + c * PIECE + q * PQ + r, group * BR + b]
                            place = (((half * NQ + q) * SIDE + c) * SLOTS + slot) * PQ + r
                            found = jnp.where(page_ids == page, place, found)
            return found

        places[...] = lax.fori_loop(0, BR, one_branch, jnp.zeros((8, 128), jnp.int32))
        copy = pltpu.make_async_copy(places, places_ref, places_sem)
        copy.start()
        copy.wait()

    feature_copies, weight_copies = [], []
    rows = hidden_ref.shape[1]

    def send_features():
        for step in range(1, MP):
            copy = pltpu.make_async_remote_copy(
                src_ref=hidden_ref, dst_ref=features.at[part],
                send_sem=feature_send.at[step - 1], recv_sem=feature_recv.at[step - 1],
                device_id=(group, shifted(part, step, MP)), device_id_type=MESH)
            copy.start()
            feature_copies.append(copy)

    def load_weights():
        for m in range(MP):
            some = pl.ds(m * rows, rows)
            copies = [
                pltpu.make_async_copy(source.at[some], target.at[some], weight_sem.at[m, i])
                for i, (source, target) in enumerate(
                    ((w_query_ref, w_query), (w_key_ref, w_key), (w_value_ref, w_value)))
            ]
            for copy in copies:
                copy.start()
            weight_copies.append(copies)

    def remote(half, q, kind, source, target, gather_at, spread_at):
        return pltpu.make_async_remote_copy(
            src_ref=source, dst_ref=target,
            send_sem=send_sem.at[half, q, kind], recv_sem=recv_sem.at[half, q, kind],
            device_id=device(half, gather_at, spread_at), device_id_type=MESH)

    spread_copies, gather_copies, forward_copies, deliver_copies = {}, {}, {}, {}
    started = []

    def pack_alive(q):
        def one(k, carry):
            branch = group * BR + jnp.minimum(alive_table[group * ALIVE + k], BR - 1)
            for half in range(2):
                where = [(spread_at, r) for spread_at in range(SIDE) for r in range(PQ)]
                pages = [table_ref[half * HALF + spread_at * PIECE + q * PQ + r, branch] for spread_at, r in where]
                blocks = [pool[page] for page in pages]
                for (spread_at, r), block in zip(where, blocks):
                    arrived[half, q, spread_at, k, r] = block
            return carry

        lax.fori_loop(0, ALIVE, one, 0)

    def spread(q):
        for half in range(2):
            a, c = along[half], across[half]
            here = pl.ds(a * 16 + c * 4, 4)
            copies = []
            for step in (2, 1, 3):
                to = shifted(c, step)
                copy = remote(
                    half, q, step - 1, arrived.at[half, q, to, pl.ds(0, ALIVE)], gathered[half][q].at[here], a, to)
                copy.start()
                copies.append(copy)
            gathered[half][q][here] = arrived[half, q, c, 0:ALIVE]
            spread_copies[half, q] = copies
            started.extend(copies)

    def gather(q):
        for half in range(2):
            a, c = along[half], across[half]
            for copy in spread_copies[half, q]:
                copy.wait_recv()
            block = gathered[half][q].at[pl.ds(a * 16, 16)]
            copies = []
            for kind, step in ((3, 1), (4, -1)):
                copy = remote(half, q, kind, block, block, shifted(a, step), c)
                copy.start()
                copies.append(copy)
            gather_copies[half, q] = copies
            started.extend(copies)

    def forward(q):
        for half in range(2):
            a, c = along[half], across[half]
            for copy in gather_copies[half, q]:
                copy.wait_recv()
            copies = []
            for kind, step, first in ((5, 1, 0), (6, -1, 8)):
                block = gathered[half][q].at[pl.ds(shifted(a, -step) * 16 + first, 8)]
                copy = remote(half, q, kind, block, block, shifted(a, step), c)
                copy.start()
                copies.append(copy)
            forward_copies[half, q] = copies
            started.extend(copies)

    def deliver(q):
        for half in range(2):
            a, c = along[half], across[half]
            for copy in forward_copies[half, q]:
                copy.wait_recv()
            deliver_copies[half, q] = []
            for step in (2, 1, 3, 0):
                to = shifted(c, step)

                def pack(batch, carry, half=half, step=step, to=to):
                    slots = [batch * BATCH + i for i in range(BATCH)]
                    sources = [source_table[(half * SIDE + to) * KIDS + j] for j in slots]
                    blocks = [gathered[half][q][source] for source in sources]
                    for j, block in zip(slots, blocks):
                        if step == 0:
                            arrived[half, q, to, ALIVE + j] = block
                        else:
                            outgoing[half, q, step - 1, j] = block
                    return carry

                lax.fori_loop(0, KIDS // BATCH, pack, 0)
                if step:
                    copy = remote(
                        half, q, 6 + step, outgoing.at[half, q, step - 1],
                        arrived.at[half, q, c, pl.ds(ALIVE, KIDS)], a, to)
                    copy.start()
                    deliver_copies[half, q].append(copy)
                    started.append(copy)

    def normalize(block, gain):
        return block * lax.rsqrt(jnp.mean(block * block, -1, keepdims=True) + 1e-06) * gain

    def project_tokens():
        for copy in small_copies[3:]:
            copy.wait()
        for copy in feature_copies:
            copy.wait_recv()
        project[...] = jnp.zeros_like(project)
        for m in range(MP):
            for copy in weight_copies[m]:
                copy.wait()
            some = pl.ds(m * rows, rows)
            part_rows = features[m]
            for i in range(4):
                columns = pl.ds(i * 256, 256)
                project[:, columns] += jnp.dot(
                    part_rows, w_query[some, columns], preferred_element_type=jnp.float32)
            project[:, pl.ds(1024, HD)] += jnp.dot(part_rows, w_key[some], preferred_element_type=jnp.float32)
            project[:, pl.ds(1152, HD)] += jnp.dot(part_rows, w_value[some], preferred_element_type=jnp.float32)
        for head in range(HEADS):
            block = normalize(project[:, pl.ds(head * HD, HD)], query_gain_ref[...]) / math.sqrt(HD)
            queries[:, head, :] = block.astype(jnp.bfloat16).astype(jnp.float32)
        key_rows = normalize(project[:, pl.ds(1024, HD)], key_gain_ref[...])
        keys[:, 0, :] = key_rows.astype(jnp.bfloat16).astype(jnp.float32)
        values[:, 0, :] = project[:, pl.ds(1152, HD)].astype(jnp.bfloat16).astype(jnp.float32)

    def start_attention():
        for slot in range(SLOTS):
            if slot < ALIVE:
                branch = jnp.minimum(alive_table[group * ALIVE + slot], BR - 1)
            else:
                branch = child_table[slot - ALIVE]
            some = pl.ds(slot * HEADS, HEADS)
            query = queries[branch]
            slot_queries[some] = query
            own_score = jnp.sum(query * keys[branch], -1, keepdims=True)
            peak[some] = jnp.broadcast_to(own_score, (HEADS, HD))
            mass[some] = jnp.ones((HEADS, HD), jnp.float32)
            mixed[some] = jnp.broadcast_to(values[branch], (HEADS, HD))

    def attend(q, first, count):
        some = pl.ds(first * HEADS, count * HEADS)
        peak[some], mass[some], mixed[some] = attend_chunk(
            arrived, slot_queries, scores, terms, mixes, peak, mass, mixed, q, first, count)

    small_copies[0].wait()
    rank_group(group, 0)
    small_copies[2].wait()
    for copy in pool_copies:
        copy.wait()
    pack_alive(0)
    pl.semaphore_wait(barrier, 2 * (SIDE - 1) + MP - 1)
    spread(0)
    for q in range(1, NQ):
        pack_alive(q)
        spread(q)
    send_features()
    load_weights()
    small_copies[1].wait()
    lax.fori_loop(0, GROUPS, rank_group, 0)
    find_sources()
    for q in range(NQ):
        gather(q)
    for q in range(NQ):
        forward(q)
    for q in range(NQ):
        deliver(q)
    invert_table()
    project_tokens()
    start_attention()
    for q in range(NQ):
        attend(q, 0, ALIVE)
    late = [copy for half in range(2) for copy in deliver_copies[half, NQ - 1]]
    for q in range(NQ - 1):
        for half in range(2):
            for copy in deliver_copies[half, q]:
                copy.wait_recv()
        attend(q, ALIVE, KIDS)
    for copy in started + feature_copies:
        if all(copy is not other for other in late):
            copy.wait_send()
    for copy in late:
        copy.wait()


def refill_kernel(
    arrived, slot_queries, peak, mass, mixed, places_ref,
    refilled_ref, attention_ref,
    refilled, scores, terms, mixes, final, result, store_sem,
):
    pages = arrived.reshape(2 * NQ * SIDE * SLOTS * PQ, PAGE, 2 * HD)
    stores = []
    for part in range(RANGES):
        def place(batch, carry, part=part):
            at = [batch * 8 + i for i in range(8)]
            places = [places_ref[part // 2, part % 2 * 64 + i] for i in at]
            blocks = [pages[place] for place in places]
            for i, block in zip(at, blocks):
                refilled[part * 64 + i] = block
            return carry

        lax.fori_loop(0, 8, place, 0)
        some = pl.ds(part * 64, 64)
        copy = pltpu.make_async_copy(refilled.at[some], refilled_ref.at[some], store_sem.at[part])
        copy.start()
        stores.append(copy)
    alive = pl.ds(0, ALIVE * HEADS)
    final[alive] = mixed[alive] / mass[alive]
    _, total, mix = attend_chunk(
        arrived, slot_queries, scores, terms, mixes, peak, mass, mixed, NQ - 1, ALIVE, KIDS)
    final[pl.ds(ALIVE * HEADS, KIDS * HEADS)] = mix / total
    for b in range(BR):
        result[b] = final[pl.ds(pl.multiple_of(places_ref[7, b] * HEADS, HEADS), HEADS)]
    for head in range(HEADS):
        attention_ref[:, pl.ds(head * HD, HD)] = result[:, head, :].astype(jnp.bfloat16)
    for copy in stores:
        copy.wait()


def shards(
    hidden, w_query, w_key, w_value, query_gain, key_gain, kv_pool, page_table, parent, surviving
):
    pool_pages = kv_pool.shape[0]
    pool = kv_pool.reshape(pool_pages, PAGE, 2 * HD)
    table = page_table.T
    vmem = pl.BlockSpec(memory_space=pltpu.VMEM)
    smem = pl.BlockSpec(memory_space=pltpu.SMEM)
    hbm = pl.BlockSpec(memory_space=pltpu.HBM)
    bf16, f32, i32 = jnp.bfloat16, jnp.float32, jnp.int32
    page_shape = (PAGE, 2 * HD)
    state = pltpu.VMEM((SLOTS * HEADS, HD), f32)
    chunk = [
        pltpu.VMEM((KIDS * HEADS, 2 * CHUNK_TOKENS), f32),
        pltpu.VMEM((KIDS * HEADS, 2 * CHUNK_TOKENS), f32),
        pltpu.VMEM((KIDS * HEADS, HD), f32),
    ]
    operands = [
        pltpu.with_memory_space_constraint(x, pltpu.HBM)
        for x in (hidden, query_gain.reshape(1, HD), key_gain.reshape(1, HD), w_query, w_key, w_value, pool,
                  table, parent, surviving)
    ]
    *kept, places = pl.pallas_call(
        relay_kernel,
        out_shape=(
            pltpu.VMEM((2, NQ, SIDE, SLOTS, PQ) + page_shape, bf16),
            state, state, state, state,
            pltpu.SMEM((8, 128), i32),
        ),
        in_specs=[hbm] * 10,
        out_specs=(vmem,) * 5 + (smem,),
        scratch_shapes=[pltpu.VMEM((GROUPS * ALIVE, PQ) + page_shape, bf16)] * (2 * NQ)
        + [
            pltpu.VMEM((2, NQ, SIDE - 1, KIDS, PQ) + page_shape, bf16),
            pltpu.VMEM(pool.shape, bf16),
            pltpu.VMEM((MP,) + hidden.shape, bf16),
            pltpu.VMEM(w_query.shape, bf16),
            pltpu.VMEM(w_key.shape, bf16),
            pltpu.VMEM(w_value.shape, bf16),
            pltpu.VMEM((BR, HEADS * HD + 2 * HD), f32),
            pltpu.VMEM((BR, HEADS, HD), f32),
            pltpu.VMEM((BR, 1, HD), f32),
            pltpu.VMEM((BR, 1, HD), f32),
            *chunk,
            pltpu.VMEM((8, 128), i32),
            pltpu.VMEM((1, HD), f32),
            pltpu.VMEM((1, HD), f32),
            pltpu.SMEM(table.shape, i32),
            pltpu.SMEM(parent.shape, i32),
            pltpu.SMEM(surviving.shape, i32),
            pltpu.SMEM((GROUPS * ALIVE,), i32),
            pltpu.SMEM((GROUPS * BR,), i32),
            pltpu.SMEM((2 * SIDE * KIDS,), i32),
            pltpu.SMEM((KIDS,), i32),
            pltpu.SMEM((BR,), i32),
            pltpu.SemaphoreType.DMA((2, NQ, 10)),
            pltpu.SemaphoreType.DMA((2, NQ, 10)),
            pltpu.SemaphoreType.DMA((MP - 1,)),
            pltpu.SemaphoreType.DMA((MP - 1,)),
            pltpu.SemaphoreType.DMA((RANGES,)),
            pltpu.SemaphoreType.DMA((MP, 3)),
            pltpu.SemaphoreType.DMA((6,)),
            pltpu.SemaphoreType.DMA,
        ],
        compiler_params=pltpu.CompilerParams(
            collective_id=0, has_side_effects=True, vmem_limit_bytes=44 * 2**20),
        name="relay_pages_and_attend",
    )(*operands)
    refilled, attention = pl.pallas_call(
        refill_kernel,
        out_shape=(
            jax.ShapeDtypeStruct(pool.shape, bf16),
            jax.ShapeDtypeStruct((BR, HEADS * HD), bf16),
        ),
        in_specs=[vmem] * 5 + [smem],
        out_specs=(hbm, vmem),
        scratch_shapes=[
            pltpu.VMEM(pool.shape, bf16),
            *chunk,
            pltpu.VMEM((SLOTS * HEADS, HD), f32),
            pltpu.VMEM((BR, HEADS, HD), f32),
            pltpu.SemaphoreType.DMA((RANGES,)),
        ],
        compiler_params=pltpu.CompilerParams(vmem_limit_bytes=44 * 2**20),
        name="refill_pool",
    )(*kept, places)
    return (refilled.reshape(kv_pool.shape), attention)


def solution(mesh):
    return jax.shard_map(
        shards,
        mesh=mesh,
        in_specs=(
            P("dp", "mp"),
            P(None, "mp"),
            P(None, "mp"),
            P(None, "mp"),
            P(),
            P(),
            P("dp", None, "mp", None),
            P(),
            P(),
            P(),
        ),
        out_specs=(P("dp", None, "mp", None), P("dp", "mp")),
        check_vma=False,
    )
```

```python
import math

import jax
import jax.numpy as jnp
from jax import lax
from jax.experimental import pallas as pl
from jax.experimental.pallas import tpu as pltpu
from jax.sharding import PartitionSpec as P

H = 64
KVH = 8
HD = 128
PAGE = 16
NPAGE = 48
BR = 16
GROUPS = 16
ALIVE = 4
KIDS = 14
SIDE = 4
NQ = 3
PQ = 2
PIECE = NQ * PQ
HALF = NPAGE // 2
MP = 8
MESH = pl.DeviceIdType.MESH
SLOTS = ALIVE + KIDS
CHUNK_TOKENS = SIDE * PQ * PAGE
HEADS = H // KVH
RANGES = 12
BATCH = 7


def attend_chunk(arrived, queries, scores, terms, mixes, peak, mass, mixed, q, first, count):
    rows = pl.ds(first * HEADS, count * HEADS)
    windows = [
        jnp.concatenate(
            [arrived[half, q, :, first + j].reshape(CHUNK_TOKENS, 2 * HD) for half in range(2)], axis=0)
        for j in range(count)
    ]
    for j in range(count):
        query = queries[pl.ds((first + j) * HEADS, HEADS)].astype(jnp.bfloat16)
        scores[pl.ds(j * HEADS, HEADS)] = lax.dot_general(
            query, windows[j][:, :HD], (((1,), (1,)), ((), ())), preferred_element_type=jnp.float32)
    part = pl.ds(0, count * HEADS)
    all_scores = scores[part]
    old = peak[rows]
    new = jnp.maximum(old, jnp.max(all_scores, -1, keepdims=True))
    scale = jnp.exp(old - new)
    all_terms = jnp.exp(all_scores - new[:, :1])
    terms[part] = all_terms
    for j in range(count):
        weights = terms[pl.ds(j * HEADS, HEADS)].astype(jnp.bfloat16)
        mixes[pl.ds(j * HEADS, HEADS)] = jnp.dot(
            weights, windows[j][:, HD:], preferred_element_type=jnp.float32)
    new_mass = mass[rows] * scale + jnp.sum(all_terms, -1, keepdims=True)
    return new, new_mass, mixed[rows] * scale + mixes[part]


def relay_kernel(
    hidden_ref, query_gain_hbm, key_gain_hbm, w_query_ref, w_key_ref, w_value_ref, pool_ref,
    table_hbm, parent_hbm, surviving_hbm,
    arrived, slot_queries, peak, mass, mixed, places_ref,
    *scratch,
):
    scratch = list(scratch)
    gathered = [[scratch.pop(0) for _ in range(NQ)] for _ in range(2)]
    (outgoing, pool, features, w_query, w_key, w_value, project, queries, keys, values,
     scores, terms, mixes, places,
     query_gain_ref, key_gain_ref, table_ref, parent_ref, surviving_ref,
     alive_table, rank_table, source_table, child_table, slot_table,
     send_sem, recv_sem, feature_send, feature_recv, pool_sem, weight_sem, small_sem, places_sem) = scratch

    group = lax.axis_index("dp")
    part = lax.axis_index("mp")
    z, y = group // SIDE, group % SIDE
    along = [z, y]
    across = [y, z]

    def device(half, gather_at, spread_at):
        if half == 0:
            return (gather_at * SIDE + spread_at, part)
        return (spread_at * SIDE + gather_at, part)

    def shifted(value, step, size=SIDE):
        return (value + step + size) % size

    pool_copy = pltpu.make_async_copy(pool_ref, pool, pool_sem)
    barrier = pltpu.get_barrier_semaphore()
    def greet_line(step, carry):
        pl.semaphore_signal(barrier, inc=1, device_id=device(0, z, shifted(y, step)), device_id_type=MESH)
        pl.semaphore_signal(barrier, inc=1, device_id=device(1, y, shifted(z, step)), device_id_type=MESH)
        return carry

    def greet_part(step, carry):
        pl.semaphore_signal(barrier, inc=1, device_id=(group, shifted(part, step, MP)), device_id_type=MESH)
        return carry

    lax.fori_loop(1, SIDE, greet_line, 0)
    lax.fori_loop(1, MP, greet_part, 0)

    small_copies = [
        pltpu.make_async_copy(source, target, small_sem.at[i])
        for i, (source, target) in enumerate((
            (surviving_hbm, surviving_ref), (parent_hbm, parent_ref), (table_hbm, table_ref),
            (query_gain_hbm, query_gain_ref), (key_gain_hbm, key_gain_ref),
            (hidden_ref, features.at[part])))
    ]
    for copy in small_copies:
        copy.start()
    pool_copy.start()

    def rank_group(at, carry):
        found = [jnp.int32(99) for _ in range(ALIVE)]
        count = jnp.int32(0)
        for branch in range(BR):
            lives = surviving_ref[at * BR + branch]
            rank_table[at * BR + branch] = count
            for k in range(ALIVE):
                found[k] = jnp.where((lives > 0) & (count == k), jnp.int32(branch), found[k])
            count = count + lives
        for k in range(ALIVE):
            alive_table[at * ALIVE + k] = found[k]
        return carry

    def child_of(at_group, j):
        branch = j
        for k in range(ALIVE):
            branch = branch + jnp.where(alive_table[at_group * ALIVE + k] - k <= j, 1, 0)
        return jnp.minimum(branch, BR - 1)

    def find_sources():
        for half in range(2):
            for spread_at in range(SIDE):
                target = z * SIDE + spread_at if half == 0 else spread_at * SIDE + y

                def find_source(j, carry, half=half, spread_at=spread_at, target=target):
                    parent = parent_ref[target * BR + child_of(target, j)]
                    from_group = parent // BR
                    rank = rank_table[parent]
                    if half == 1:
                        from_group = (from_group % SIDE) * SIDE + from_group // SIDE
                    source_table[(half * SIDE + spread_at) * KIDS + j] = from_group * ALIVE + rank
                    return carry

                lax.fori_loop(0, KIDS, find_source, 0)

        def own_children(j, carry):
            child_table[j] = child_of(group, j)
            return carry

        lax.fori_loop(0, KIDS, own_children, 0)

        def own_slots(b, carry):
            rank = rank_table[group * BR + b]
            lives = surviving_ref[group * BR + b]
            slot_table[b] = jnp.minimum(jnp.where(lives > 0, rank, ALIVE + b - rank), SLOTS - 1)
            return carry

        lax.fori_loop(0, BR, own_slots, 0)

    def invert_table():
        row = lax.broadcasted_iota(jnp.int32, (8, 128), 0)
        lane = lax.broadcasted_iota(jnp.int32, (8, 128), 1)
        page_ids = row * 128 + lane

        def one_branch(b, found):
            slot = slot_table[b]
            found = jnp.where((row == 7) & (lane == b), slot, found)
            for half in range(2):
                for c in range(SIDE):
                    for q in range(NQ):
                        for r in range(PQ):
                            page = table_ref[half * HALF + c * PIECE + q * PQ + r, group * BR + b]
                            place = (((half * NQ + q) * SIDE + c) * SLOTS + slot) * PQ + r
                            found = jnp.where(page_ids == page, place, found)
            return found

        places[...] = lax.fori_loop(0, BR, one_branch, jnp.zeros((8, 128), jnp.int32))
        copy = pltpu.make_async_copy(places, places_ref, places_sem)
        copy.start()
        copy.wait()

    feature_copies, weight_copies = [], []
    rows = hidden_ref.shape[1]

    def send_features():
        for step in range(1, MP):
            copy = pltpu.make_async_remote_copy(
                src_ref=hidden_ref, dst_ref=features.at[part],
                send_sem=feature_send.at[step - 1], recv_sem=feature_recv.at[step - 1],
                device_id=(group, shifted(part, step, MP)), device_id_type=MESH)
            copy.start()
            feature_copies.append(copy)

    def load_weights():
        for m in range(MP):
            some = pl.ds(m * rows, rows)
            copies = [
                pltpu.make_async_copy(source.at[some], target.at[some], weight_sem.at[m, i])
                for i, (source, target) in enumerate(
                    ((w_query_ref, w_query), (w_key_ref, w_key), (w_value_ref, w_value)))
            ]
            for copy in copies:
                copy.start()
            weight_copies.append(copies)

    def remote(half, q, kind, source, target, gather_at, spread_at):
        return pltpu.make_async_remote_copy(
            src_ref=source, dst_ref=target,
            send_sem=send_sem.at[half, q, kind], recv_sem=recv_sem.at[half, q, kind],
            device_id=device(half, gather_at, spread_at), device_id_type=MESH)

    spread_copies, gather_copies, forward_copies, deliver_copies = {}, {}, {}, {}
    started = []

    def pack_alive(q):
        def one(k, carry):
            branch = group * BR + jnp.minimum(alive_table[group * ALIVE + k], BR - 1)
            for half in range(2):
                where = [(spread_at, r) for spread_at in range(SIDE) for r in range(PQ)]
                pages = [table_ref[half * HALF + spread_at * PIECE + q * PQ + r, branch] for spread_at, r in where]
                blocks = [pool[page] for page in pages]
                for (spread_at, r), block in zip(where, blocks):
                    arrived[half, q, spread_at, k, r] = block
            return carry

        lax.fori_loop(0, ALIVE, one, 0)

    def spread(q):
        for half in range(2):
            a, c = along[half], across[half]
            here = pl.ds(a * 16 + c * 4, 4)
            copies = []
            for step in (2, 1, 3):
                to = shifted(c, step)
                copy = remote(
                    half, q, step - 1, arrived.at[half, q, to, pl.ds(0, ALIVE)], gathered[half][q].at[here], a, to)
                copy.start()
                copies.append(copy)
            gathered[half][q][here] = arrived[half, q, c, 0:ALIVE]
            spread_copies[half, q] = copies
            started.extend(copies)

    def gather(q):
        for half in range(2):
            a, c = along[half], across[half]
            for copy in spread_copies[half, q]:
                copy.wait_recv()
            block = gathered[half][q].at[pl.ds(a * 16, 16)]
            copies = []
            for kind, step in ((3, 1), (4, -1)):
                copy = remote(half, q, kind, block, block, shifted(a, step), c)
                copy.start()
                copies.append(copy)
            gather_copies[half, q] = copies
            started.extend(copies)

    def forward(q):
        for half in range(2):
            a, c = along[half], across[half]
            for copy in gather_copies[half, q]:
                copy.wait_recv()
            copies = []
            for kind, step, first in ((5, 1, 0), (6, -1, 8)):
                block = gathered[half][q].at[pl.ds(shifted(a, -step) * 16 + first, 8)]
                copy = remote(half, q, kind, block, block, shifted(a, step), c)
                copy.start()
                copies.append(copy)
            forward_copies[half, q] = copies
            started.extend(copies)

    def deliver(q):
        for half in range(2):
            a, c = along[half], across[half]
            for copy in forward_copies[half, q]:
                copy.wait_recv()
            deliver_copies[half, q] = []
            for step in (2, 1, 3, 0):
                to = shifted(c, step)

                def pack(batch, carry, half=half, step=step, to=to):
                    slots = [batch * BATCH + i for i in range(BATCH)]
                    sources = [source_table[(half * SIDE + to) * KIDS + j] for j in slots]
                    blocks = [gathered[half][q][source] for source in sources]
                    for j, block in zip(slots, blocks):
                        if step == 0:
                            arrived[half, q, to, ALIVE + j] = block
                        else:
                            outgoing[half, q, step - 1, j] = block
                    return carry

                lax.fori_loop(0, KIDS // BATCH, pack, 0)
                if step:
                    copy = remote(
                        half, q, 6 + step, outgoing.at[half, q, step - 1],
                        arrived.at[half, q, c, pl.ds(ALIVE, KIDS)], a, to)
                    copy.start()
                    deliver_copies[half, q].append(copy)
                    started.append(copy)

    def normalize(block, gain):
        return block * lax.rsqrt(jnp.mean(block * block, -1, keepdims=True) + 1e-06) * gain

    def project_tokens():
        for copy in small_copies[3:]:
            copy.wait()
        for copy in feature_copies:
            copy.wait_recv()
        project[...] = jnp.zeros_like(project)
        for m in range(MP):
            for copy in weight_copies[m]:
                copy.wait()
            some = pl.ds(m * rows, rows)
            part_rows = features[m]
            for i in range(4):
                columns = pl.ds(i * 256, 256)
                project[:, columns] += jnp.dot(
                    part_rows, w_query[some, columns], preferred_element_type=jnp.float32)
            project[:, pl.ds(1024, HD)] += jnp.dot(part_rows, w_key[some], preferred_element_type=jnp.float32)
            project[:, pl.ds(1152, HD)] += jnp.dot(part_rows, w_value[some], preferred_element_type=jnp.float32)
        for head in range(HEADS):
            block = normalize(project[:, pl.ds(head * HD, HD)], query_gain_ref[...]) / math.sqrt(HD)
            queries[:, head, :] = block.astype(jnp.bfloat16).astype(jnp.float32)
        key_rows = normalize(project[:, pl.ds(1024, HD)], key_gain_ref[...])
        keys[:, 0, :] = key_rows.astype(jnp.bfloat16).astype(jnp.float32)
        values[:, 0, :] = project[:, pl.ds(1152, HD)].astype(jnp.bfloat16).astype(jnp.float32)

    def start_attention():
        for slot in range(SLOTS):
            if slot < ALIVE:
                branch = jnp.minimum(alive_table[group * ALIVE + slot], BR - 1)
            else:
                branch = child_table[slot - ALIVE]
            some = pl.ds(slot * HEADS, HEADS)
            query = queries[branch]
            slot_queries[some] = query
            own_score = jnp.sum(query * keys[branch], -1, keepdims=True)
            peak[some] = jnp.broadcast_to(own_score, (HEADS, HD))
            mass[some] = jnp.ones((HEADS, HD), jnp.float32)
            mixed[some] = jnp.broadcast_to(values[branch], (HEADS, HD))

    def attend(q, first, count):
        some = pl.ds(first * HEADS, count * HEADS)
        peak[some], mass[some], mixed[some] = attend_chunk(
            arrived, slot_queries, scores, terms, mixes, peak, mass, mixed, q, first, count)

    small_copies[0].wait()
    rank_group(group, 0)
    small_copies[2].wait()
    pool_copy.wait()
    pack_alive(0)
    pl.semaphore_wait(barrier, 2 * (SIDE - 1) + MP - 1)
    spread(0)
    for q in range(1, NQ):
        pack_alive(q)
        spread(q)
    send_features()
    load_weights()
    small_copies[1].wait()
    lax.fori_loop(0, GROUPS, rank_group, 0)
    find_sources()
    for q in range(NQ):
        gather(q)
    for q in range(NQ):
        forward(q)
    for q in range(NQ):
        deliver(q)
    invert_table()
    project_tokens()
    start_attention()
    for q in range(NQ):
        attend(q, 0, ALIVE)
    late = [copy for half in range(2) for copy in deliver_copies[half, NQ - 1]]
    for q in range(NQ - 1):
        for half in range(2):
            for copy in deliver_copies[half, q]:
                copy.wait_recv()
        attend(q, ALIVE, KIDS)
    for copy in started + feature_copies:
        if all(copy is not other for other in late):
            copy.wait_send()
    for copy in late:
        copy.wait()


def refill_kernel(
    arrived, slot_queries, peak, mass, mixed, places_ref,
    refilled_ref, attention_ref,
    refilled, scores, terms, mixes, final, result, store_sem,
):
    pages = arrived.reshape(2 * NQ * SIDE * SLOTS * PQ, PAGE, 2 * HD)
    stores = [
        pltpu.make_async_copy(
            refilled.at[pl.ds(part * 64, 64)], refilled_ref.at[pl.ds(part * 64, 64)], store_sem.at[part])
        for part in range(RANGES)
    ]

    def place(part, carry):
        for batch in range(4):
            at = [batch * 16 + i for i in range(16)]
            places = [places_ref[part // 2, part % 2 * 64 + i] for i in at]
            blocks = [pages[place] for place in places]
            for i, block in zip(at, blocks):
                refilled[part * 64 + i] = block
        some = pl.ds(part * 64, 64)
        pltpu.make_async_copy(refilled.at[some], refilled_ref.at[some], store_sem.at[part]).start()
        return carry

    lax.fori_loop(0, RANGES, place, 0)
    alive = pl.ds(0, ALIVE * HEADS)
    final[alive] = mixed[alive] / mass[alive]
    _, total, mix = attend_chunk(
        arrived, slot_queries, scores, terms, mixes, peak, mass, mixed, NQ - 1, ALIVE, KIDS)
    final[pl.ds(ALIVE * HEADS, KIDS * HEADS)] = mix / total
    for b in range(BR):
        result[b] = final[pl.ds(pl.multiple_of(places_ref[7, b] * HEADS, HEADS), HEADS)]
    for head in range(HEADS):
        attention_ref[:, pl.ds(head * HD, HD)] = result[:, head, :].astype(jnp.bfloat16)
    for copy in stores:
        copy.wait()


def shards(
    hidden, w_query, w_key, w_value, query_gain, key_gain, kv_pool, page_table, parent, surviving
):
    pool_pages = kv_pool.shape[0]
    pool = kv_pool.reshape(pool_pages, PAGE, 2 * HD)
    table = page_table.T
    vmem = pl.BlockSpec(memory_space=pltpu.VMEM)
    smem = pl.BlockSpec(memory_space=pltpu.SMEM)
    hbm = pl.BlockSpec(memory_space=pltpu.HBM)
    bf16, f32, i32 = jnp.bfloat16, jnp.float32, jnp.int32
    page_shape = (PAGE, 2 * HD)
    state = pltpu.VMEM((SLOTS * HEADS, HD), f32)
    chunk = [
        pltpu.VMEM((KIDS * HEADS, 2 * CHUNK_TOKENS), f32),
        pltpu.VMEM((KIDS * HEADS, 2 * CHUNK_TOKENS), f32),
        pltpu.VMEM((KIDS * HEADS, HD), f32),
    ]
    operands = [
        pltpu.with_memory_space_constraint(x, pltpu.HBM)
        for x in (hidden, query_gain.reshape(1, HD), key_gain.reshape(1, HD), w_query, w_key, w_value, pool,
                  table, parent, surviving)
    ]
    *kept, places = pl.pallas_call(
        relay_kernel,
        out_shape=(
            pltpu.VMEM((2, NQ, SIDE, SLOTS, PQ) + page_shape, bf16),
            state, state, state, state,
            pltpu.SMEM((8, 128), i32),
        ),
        in_specs=[hbm] * 10,
        out_specs=(vmem,) * 5 + (smem,),
        scratch_shapes=[pltpu.VMEM((GROUPS * ALIVE, PQ) + page_shape, bf16)] * (2 * NQ)
        + [
            pltpu.VMEM((2, NQ, SIDE - 1, KIDS, PQ) + page_shape, bf16),
            pltpu.VMEM(pool.shape, bf16),
            pltpu.VMEM((MP,) + hidden.shape, bf16),
            pltpu.VMEM(w_query.shape, bf16),
            pltpu.VMEM(w_key.shape, bf16),
            pltpu.VMEM(w_value.shape, bf16),
            pltpu.VMEM((BR, HEADS * HD + 2 * HD), f32),
            pltpu.VMEM((BR, HEADS, HD), f32),
            pltpu.VMEM((BR, 1, HD), f32),
            pltpu.VMEM((BR, 1, HD), f32),
            *chunk,
            pltpu.VMEM((8, 128), i32),
            pltpu.VMEM((1, HD), f32),
            pltpu.VMEM((1, HD), f32),
            pltpu.SMEM(table.shape, i32),
            pltpu.SMEM(parent.shape, i32),
            pltpu.SMEM(surviving.shape, i32),
            pltpu.SMEM((GROUPS * ALIVE,), i32),
            pltpu.SMEM((GROUPS * BR,), i32),
            pltpu.SMEM((2 * SIDE * KIDS,), i32),
            pltpu.SMEM((KIDS,), i32),
            pltpu.SMEM((BR,), i32),
            pltpu.SemaphoreType.DMA((2, NQ, 10)),
            pltpu.SemaphoreType.DMA((2, NQ, 10)),
            pltpu.SemaphoreType.DMA((MP - 1,)),
            pltpu.SemaphoreType.DMA((MP - 1,)),
            pltpu.SemaphoreType.DMA,
            pltpu.SemaphoreType.DMA((MP, 3)),
            pltpu.SemaphoreType.DMA((6,)),
            pltpu.SemaphoreType.DMA,
        ],
        compiler_params=pltpu.CompilerParams(
            collective_id=0, has_side_effects=True, vmem_limit_bytes=44 * 2**20),
        name="relay_pages_and_attend",
    )(*operands)
    refilled, attention = pl.pallas_call(
        refill_kernel,
        out_shape=(
            jax.ShapeDtypeStruct(pool.shape, bf16),
            jax.ShapeDtypeStruct((BR, HEADS * HD), bf16),
        ),
        in_specs=[vmem] * 5 + [smem],
        out_specs=(hbm, vmem),
        scratch_shapes=[
            pltpu.VMEM(pool.shape, bf16),
            *chunk,
            pltpu.VMEM((SLOTS * HEADS, HD), f32),
            pltpu.VMEM((BR, HEADS, HD), f32),
            pltpu.SemaphoreType.DMA((RANGES,)),
        ],
        compiler_params=pltpu.CompilerParams(vmem_limit_bytes=44 * 2**20),
        name="refill_pool",
    )(*kept, places)
    return (refilled.reshape(kv_pool.shape), attention)


def solution(mesh):
    return jax.shard_map(
        shards,
        mesh=mesh,
        in_specs=(
            P("dp", "mp"),
            P(None, "mp"),
            P(None, "mp"),
            P(None, "mp"),
            P(),
            P(),
            P("dp", None, "mp", None),
            P(),
            P(),
            P(),
        ),
        out_specs=(P("dp", None, "mp", None), P("dp", "mp")),
        check_vma=False,
    )
```

```python
import math

import jax
import jax.numpy as jnp
from jax import lax
from jax.experimental import pallas as pl
from jax.experimental.pallas import tpu as pltpu
from jax.sharding import PartitionSpec as P

H = 64
KVH = 8
HD = 128
PAGE = 16
NPAGE = 48
BR = 16
GROUPS = 16
ALIVE = 4
KIDS = 14
SIDE = 4
NQ = 2
PQ = 3
PIECE = NQ * PQ
HALF = NPAGE // 2
MP = 8
MESH = pl.DeviceIdType.MESH
SLOTS = ALIVE + KIDS
CHUNK_TOKENS = SIDE * PQ * PAGE
HEADS = H // KVH
RANGES = 12
BATCH = 7


def attend_chunk(arrived, queries, scores, terms, mixes, peak, mass, mixed, q, first, count):
    rows = pl.ds(first * HEADS, count * HEADS)
    windows = [
        jnp.concatenate(
            [arrived[half, q, :, first + j].reshape(CHUNK_TOKENS, 2 * HD) for half in range(2)], axis=0)
        for j in range(count)
    ]
    for j in range(count):
        query = queries[pl.ds((first + j) * HEADS, HEADS)].astype(jnp.bfloat16)
        scores[pl.ds(j * HEADS, HEADS)] = lax.dot_general(
            query, windows[j][:, :HD], (((1,), (1,)), ((), ())), preferred_element_type=jnp.float32)
    part = pl.ds(0, count * HEADS)
    all_scores = scores[part]
    old = peak[rows]
    new = jnp.maximum(old, jnp.max(all_scores, -1, keepdims=True))
    scale = jnp.exp(old - new)
    all_terms = jnp.exp(all_scores - new[:, :1])
    terms[part] = all_terms
    for j in range(count):
        weights = terms[pl.ds(j * HEADS, HEADS)].astype(jnp.bfloat16)
        mixes[pl.ds(j * HEADS, HEADS)] = jnp.dot(
            weights, windows[j][:, HD:], preferred_element_type=jnp.float32)
    new_mass = mass[rows] * scale + jnp.sum(all_terms, -1, keepdims=True)
    return new, new_mass, mixed[rows] * scale + mixes[part]


def relay_kernel(
    hidden_ref, query_gain_hbm, key_gain_hbm, w_query_ref, w_key_ref, w_value_ref, pool_ref,
    table_hbm, parent_hbm, surviving_hbm,
    arrived, slot_queries, peak, mass, mixed, places_ref,
    *scratch,
):
    scratch = list(scratch)
    gathered = [scratch.pop(0) for _ in range(NQ)]
    (outgoing, pool, features, w_query, w_key, w_value, project, queries, keys, values,
     scores, terms, mixes, places,
     query_gain_ref, key_gain_ref, table_ref, parent_ref, surviving_ref,
     alive_table, rank_table, source_table, child_table, slot_table,
     send_sem, recv_sem, feature_send, feature_recv, pool_sem, weight_sem, small_sem, places_sem) = scratch

    group = lax.axis_index("dp")
    part = lax.axis_index("mp")
    z, y = group // SIDE, group % SIDE

    def device(half, gather_at, spread_at):
        if half == 0:
            return (gather_at * SIDE + spread_at, part)
        return (spread_at * SIDE + gather_at, part)

    def shifted(value, step, size=SIDE):
        return (value + step + size) % size

    pool_copy = pltpu.make_async_copy(pool_ref, pool, pool_sem)
    barrier = pltpu.get_barrier_semaphore()
    def greet_line(step, carry):
        pl.semaphore_signal(barrier, inc=1, device_id=device(0, z, shifted(y, step)), device_id_type=MESH)
        pl.semaphore_signal(barrier, inc=1, device_id=device(1, y, shifted(z, step)), device_id_type=MESH)
        return carry

    def greet_part(step, carry):
        pl.semaphore_signal(barrier, inc=1, device_id=(group, shifted(part, step, MP)), device_id_type=MESH)
        return carry

    lax.fori_loop(1, SIDE, greet_line, 0)
    lax.fori_loop(1, MP, greet_part, 0)

    small_copies = [
        pltpu.make_async_copy(source, target, small_sem.at[i])
        for i, (source, target) in enumerate((
            (surviving_hbm, surviving_ref), (parent_hbm, parent_ref), (table_hbm, table_ref),
            (query_gain_hbm, query_gain_ref), (key_gain_hbm, key_gain_ref),
            (hidden_ref, features.at[part])))
    ]
    for copy in small_copies:
        copy.start()
    pool_copy.start()

    def rank_group(at, carry):
        found = [jnp.int32(99) for _ in range(ALIVE)]
        count = jnp.int32(0)
        for branch in range(BR):
            lives = surviving_ref[at * BR + branch]
            rank_table[at * BR + branch] = count
            for k in range(ALIVE):
                found[k] = jnp.where((lives > 0) & (count == k), jnp.int32(branch), found[k])
            count = count + lives
        for k in range(ALIVE):
            alive_table[at * ALIVE + k] = found[k]
        return carry

    def child_of(at_group, j):
        branch = j
        for k in range(ALIVE):
            branch = branch + jnp.where(alive_table[at_group * ALIVE + k] - k <= j, 1, 0)
        return jnp.minimum(branch, BR - 1)

    def find_sources():
        for half in range(2):
            for spread_at in range(SIDE):
                target = z * SIDE + spread_at if half == 0 else spread_at * SIDE + y

                def find_source(j, carry, half=half, spread_at=spread_at, target=target):
                    parent = parent_ref[target * BR + child_of(target, j)]
                    from_group = parent // BR
                    rank = rank_table[parent]
                    if half == 1:
                        from_group = (from_group % SIDE) * SIDE + from_group // SIDE
                    source_table[(half * SIDE + spread_at) * KIDS + j] = (half * GROUPS + from_group) * ALIVE + rank
                    return carry

                lax.fori_loop(0, KIDS, find_source, 0)

        def own_children(j, carry):
            child_table[j] = child_of(group, j)
            return carry

        lax.fori_loop(0, KIDS, own_children, 0)

        def own_slots(b, carry):
            rank = rank_table[group * BR + b]
            lives = surviving_ref[group * BR + b]
            slot_table[b] = jnp.minimum(jnp.where(lives > 0, rank, ALIVE + b - rank), SLOTS - 1)
            return carry

        lax.fori_loop(0, BR, own_slots, 0)

    def invert_table():
        row = lax.broadcasted_iota(jnp.int32, (8, 128), 0)
        lane = lax.broadcasted_iota(jnp.int32, (8, 128), 1)
        page_ids = row * 128 + lane

        def one_branch(b, found):
            slot = slot_table[b]
            found = jnp.where((row == 7) & (lane == b), slot, found)
            for half in range(2):
                for c in range(SIDE):
                    for q in range(NQ):
                        for r in range(PQ):
                            page = table_ref[half * HALF + c * PIECE + q * PQ + r, group * BR + b]
                            place = (((half * NQ + q) * SIDE + c) * SLOTS + slot) * PQ + r
                            found = jnp.where(page_ids == page, place, found)
            return found

        places[...] = lax.fori_loop(0, BR, one_branch, jnp.zeros((8, 128), jnp.int32))
        copy = pltpu.make_async_copy(places, places_ref, places_sem)
        copy.start()
        copy.wait()

    feature_copies, weight_copies = [], []
    rows = hidden_ref.shape[1]

    def send_features():
        for step in range(1, MP):
            copy = pltpu.make_async_remote_copy(
                src_ref=hidden_ref, dst_ref=features.at[part],
                send_sem=feature_send.at[step - 1], recv_sem=feature_recv.at[step - 1],
                device_id=(group, shifted(part, step, MP)), device_id_type=MESH)
            copy.start()
            feature_copies.append(copy)

    def load_weights():
        for m in range(MP):
            some = pl.ds(m * rows, rows)
            copies = [
                pltpu.make_async_copy(source.at[some], target.at[some], weight_sem.at[m, i])
                for i, (source, target) in enumerate(
                    ((w_query_ref, w_query), (w_key_ref, w_key), (w_value_ref, w_value)))
            ]
            for copy in copies:
                copy.start()
            weight_copies.append(copies)

    def remote(half, q, kind, source, target, gather_at, spread_at):
        to = jnp.where(half == 0, gather_at * SIDE + spread_at, spread_at * SIDE + gather_at)
        return pltpu.make_async_remote_copy(
            src_ref=source, dst_ref=target,
            send_sem=send_sem.at[half, q, kind], recv_sem=recv_sem.at[half, q, kind],
            device_id=(to, part), device_id_type=MESH)

    def place_of(half):
        return jnp.where(half == 0, z, y), jnp.where(half == 0, y, z)

    def each_half(body):
        def run(half, carry):
            body(half, *place_of(half))
            return carry

        lax.fori_loop(0, 2, run, 0)

    def each_step(first, last, body):
        def run(step, carry):
            body(step)
            return carry

        lax.fori_loop(first, last, run, 0)

    def pack_alive(q):
        def one(k, carry):
            branch = group * BR + jnp.minimum(alive_table[group * ALIVE + k], BR - 1)
            for half in range(2):
                where = [(spread_at, r) for spread_at in range(SIDE) for r in range(PQ)]
                pages = [table_ref[half * HALF + spread_at * PIECE + q * PQ + r, branch] for spread_at, r in where]
                blocks = [pool[page] for page in pages]
                for (spread_at, r), block in zip(where, blocks):
                    arrived[half, q, spread_at, k, r] = block
            return carry

        lax.fori_loop(0, ALIVE, one, 0)

    def spread_copy(q, half, a, c, step):
        to = shifted(c, step)
        here = pl.ds(half * 64 + a * 16 + c * 4, 4)
        return remote(
            half, q, step - 1, arrived.at[half, q, to, pl.ds(0, ALIVE)], gathered[q].at[here], a, to)

    def spread(q):
        def one(half, a, c):
            each_step(1, SIDE, lambda step: spread_copy(q, half, a, c, step).start())
            gathered[q][pl.ds(half * 64 + a * 16 + c * 4, 4)] = arrived[half, q, c, 0:ALIVE]

        each_half(one)

    def gather_copy(q, half, a, c, way):
        block = gathered[q].at[pl.ds(half * 64 + a * 16, 16)]
        return remote(half, q, 3 + way, block, block, shifted(a, 1 - 2 * way), c)

    def gather(q):
        def one(half, a, c):
            each_step(1, SIDE, lambda step: spread_copy(q, half, a, c, step).wait_recv())
            each_step(0, 2, lambda way: gather_copy(q, half, a, c, way).start())

        each_half(one)

    def forward_copy(q, half, a, c, way):
        step = 1 - 2 * way
        block = gathered[q].at[pl.ds(half * 64 + shifted(a, -step) * 16 + way * 8, 8)]
        return remote(half, q, 5 + way, block, block, shifted(a, step), c)

    def forward(q):
        def one(half, a, c):
            each_step(0, 2, lambda way: gather_copy(q, half, a, c, way).wait_recv())
            each_step(0, 2, lambda way: forward_copy(q, half, a, c, way).start())

        each_half(one)

    def deliver_copy(q, half, a, c, step):
        return remote(
            half, q, 6 + step, outgoing.at[half, q, step - 1],
            arrived.at[half, q, c, pl.ds(ALIVE, KIDS)], a, shifted(c, step))

    def deliver(q):
        each_half(lambda half, a, c: each_step(
            0, 2, lambda way: forward_copy(q, half, a, c, way).wait_recv()))

        def one(half, a, c):
            def pack(to, put):
                def few(batch, carry):
                    slots = [batch * BATCH + i for i in range(BATCH)]
                    sources = [source_table[(half * SIDE + to) * KIDS + j] for j in slots]
                    blocks = [gathered[q][source] for source in sources]
                    for j, block in zip(slots, blocks):
                        put(j, block)
                    return carry

                lax.fori_loop(0, KIDS // BATCH, few, 0)

            def send(step):
                def put(j, block):
                    outgoing[half, q, step - 1, j] = block

                pack(shifted(c, step), put)
                deliver_copy(q, half, a, c, step).start()

            def keep(j, block):
                arrived[half, q, c, ALIVE + j] = block

            each_step(1, SIDE, send)
            pack(c, keep)

        each_half(one)

    def wait_delivered(q):
        each_half(lambda half, a, c: each_step(
            1, SIDE, lambda step: deliver_copy(q, half, a, c, step).wait_recv()))

    def wait_sent(q):
        def one(half, a, c):
            each_step(1, SIDE, lambda step: spread_copy(q, half, a, c, step).wait_send())
            each_step(0, 2, lambda way: gather_copy(q, half, a, c, way).wait_send())
            each_step(0, 2, lambda way: forward_copy(q, half, a, c, way).wait_send())

        each_half(one)

    def wait_delivery_sent(q):
        each_half(lambda half, a, c: each_step(
            1, SIDE, lambda step: deliver_copy(q, half, a, c, step).wait_send()))

    def normalize(block, gain):
        return block * lax.rsqrt(jnp.mean(block * block, -1, keepdims=True) + 1e-06) * gain

    def project_tokens():
        for copy in small_copies[3:]:
            copy.wait()
        for copy in feature_copies:
            copy.wait_recv()
        project[...] = jnp.zeros_like(project)
        for m in range(MP):
            for copy in weight_copies[m]:
                copy.wait()
            some = pl.ds(m * rows, rows)
            part_rows = features[m]
            for i in range(4):
                columns = pl.ds(i * 256, 256)
                project[:, columns] += jnp.dot(
                    part_rows, w_query[some, columns], preferred_element_type=jnp.float32)
            project[:, pl.ds(1024, HD)] += jnp.dot(part_rows, w_key[some], preferred_element_type=jnp.float32)
            project[:, pl.ds(1152, HD)] += jnp.dot(part_rows, w_value[some], preferred_element_type=jnp.float32)
        for head in range(HEADS):
            block = normalize(project[:, pl.ds(head * HD, HD)], query_gain_ref[...]) / math.sqrt(HD)
            queries[:, head, :] = block.astype(jnp.bfloat16).astype(jnp.float32)
        key_rows = normalize(project[:, pl.ds(1024, HD)], key_gain_ref[...])
        keys[:, 0, :] = key_rows.astype(jnp.bfloat16).astype(jnp.float32)
        values[:, 0, :] = project[:, pl.ds(1152, HD)].astype(jnp.bfloat16).astype(jnp.float32)

    def start_attention():
        for slot in range(SLOTS):
            if slot < ALIVE:
                branch = jnp.minimum(alive_table[group * ALIVE + slot], BR - 1)
            else:
                branch = child_table[slot - ALIVE]
            some = pl.ds(slot * HEADS, HEADS)
            query = queries[branch]
            slot_queries[some] = query
            own_score = jnp.sum(query * keys[branch], -1, keepdims=True)
            peak[some] = jnp.broadcast_to(own_score, (HEADS, HD))
            mass[some] = jnp.ones((HEADS, HD), jnp.float32)
            mixed[some] = jnp.broadcast_to(values[branch], (HEADS, HD))

    def attend(q, first, count):
        some = pl.ds(first * HEADS, count * HEADS)
        peak[some], mass[some], mixed[some] = attend_chunk(
            arrived, slot_queries, scores, terms, mixes, peak, mass, mixed, q, first, count)

    small_copies[0].wait()
    rank_group(group, 0)
    small_copies[2].wait()
    pool_copy.wait()
    pack_alive(0)
    pl.semaphore_wait(barrier, 2 * (SIDE - 1) + MP - 1)
    spread(0)
    for q in range(1, NQ):
        pack_alive(q)
        spread(q)
    send_features()
    load_weights()
    small_copies[1].wait()
    lax.fori_loop(0, GROUPS, rank_group, 0)
    find_sources()
    for q in range(NQ):
        gather(q)
    for q in range(NQ):
        forward(q)
    for q in range(NQ):
        deliver(q)
    invert_table()
    project_tokens()
    start_attention()
    for q in range(NQ):
        attend(q, 0, ALIVE)
    for q in range(NQ - 1):
        wait_delivered(q)
        attend(q, ALIVE, KIDS)
    for q in range(NQ):
        wait_sent(q)
        if q < NQ - 1:
            wait_delivery_sent(q)
    for copy in feature_copies:
        copy.wait_send()
    wait_delivered(NQ - 1)
    wait_delivery_sent(NQ - 1)


def refill_kernel(
    arrived, slot_queries, peak, mass, mixed, places_ref,
    refilled_ref, attention_ref,
    refilled, scores, terms, mixes, final, result, store_sem,
):
    pages = arrived.reshape(2 * NQ * SIDE * SLOTS * PQ, PAGE, 2 * HD)
    stores = [
        pltpu.make_async_copy(
            refilled.at[pl.ds(part * 64, 64)], refilled_ref.at[pl.ds(part * 64, 64)], store_sem.at[part])
        for part in range(RANGES)
    ]

    def place(part, carry):
        for batch in range(4):
            at = [batch * 16 + i for i in range(16)]
            places = [places_ref[part // 2, part % 2 * 64 + i] for i in at]
            blocks = [pages[place] for place in places]
            for i, block in zip(at, blocks):
                refilled[part * 64 + i] = block
        some = pl.ds(part * 64, 64)
        pltpu.make_async_copy(refilled.at[some], refilled_ref.at[some], store_sem.at[part]).start()
        return carry

    lax.fori_loop(0, RANGES, place, 0)
    alive = pl.ds(0, ALIVE * HEADS)
    final[alive] = mixed[alive] / mass[alive]
    _, total, mix = attend_chunk(
        arrived, slot_queries, scores, terms, mixes, peak, mass, mixed, NQ - 1, ALIVE, KIDS)
    final[pl.ds(ALIVE * HEADS, KIDS * HEADS)] = mix / total
    for b in range(BR):
        result[b] = final[pl.ds(pl.multiple_of(places_ref[7, b] * HEADS, HEADS), HEADS)]
    for head in range(HEADS):
        attention_ref[:, pl.ds(head * HD, HD)] = result[:, head, :].astype(jnp.bfloat16)
    for copy in stores:
        copy.wait()


def shards(
    hidden, w_query, w_key, w_value, query_gain, key_gain, kv_pool, page_table, parent, surviving
):
    pool_pages = kv_pool.shape[0]
    pool = kv_pool.reshape(pool_pages, PAGE, 2 * HD)
    table = page_table.T
    vmem = pl.BlockSpec(memory_space=pltpu.VMEM)
    smem = pl.BlockSpec(memory_space=pltpu.SMEM)
    hbm = pl.BlockSpec(memory_space=pltpu.HBM)
    bf16, f32, i32 = jnp.bfloat16, jnp.float32, jnp.int32
    page_shape = (PAGE, 2 * HD)
    state = pltpu.VMEM((SLOTS * HEADS, HD), f32)
    chunk = [
        pltpu.VMEM((KIDS * HEADS, 2 * CHUNK_TOKENS), f32),
        pltpu.VMEM((KIDS * HEADS, 2 * CHUNK_TOKENS), f32),
        pltpu.VMEM((KIDS * HEADS, HD), f32),
    ]
    operands = [
        pltpu.with_memory_space_constraint(x, pltpu.HBM)
        for x in (hidden, query_gain.reshape(1, HD), key_gain.reshape(1, HD), w_query, w_key, w_value, pool,
                  table, parent, surviving)
    ]
    *kept, places = pl.pallas_call(
        relay_kernel,
        out_shape=(
            pltpu.VMEM((2, NQ, SIDE, SLOTS, PQ) + page_shape, bf16),
            state, state, state, state,
            pltpu.SMEM((8, 128), i32),
        ),
        in_specs=[hbm] * 10,
        out_specs=(vmem,) * 5 + (smem,),
        scratch_shapes=[pltpu.VMEM((2 * GROUPS * ALIVE, PQ) + page_shape, bf16)] * NQ
        + [
            pltpu.VMEM((2, NQ, SIDE - 1, KIDS, PQ) + page_shape, bf16),
            pltpu.VMEM(pool.shape, bf16),
            pltpu.VMEM((MP,) + hidden.shape, bf16),
            pltpu.VMEM(w_query.shape, bf16),
            pltpu.VMEM(w_key.shape, bf16),
            pltpu.VMEM(w_value.shape, bf16),
            pltpu.VMEM((BR, HEADS * HD + 2 * HD), f32),
            pltpu.VMEM((BR, HEADS, HD), f32),
            pltpu.VMEM((BR, 1, HD), f32),
            pltpu.VMEM((BR, 1, HD), f32),
            *chunk,
            pltpu.VMEM((8, 128), i32),
            pltpu.VMEM((1, HD), f32),
            pltpu.VMEM((1, HD), f32),
            pltpu.SMEM(table.shape, i32),
            pltpu.SMEM(parent.shape, i32),
            pltpu.SMEM(surviving.shape, i32),
            pltpu.SMEM((GROUPS * ALIVE,), i32),
            pltpu.SMEM((GROUPS * BR,), i32),
            pltpu.SMEM((2 * SIDE * KIDS,), i32),
            pltpu.SMEM((KIDS,), i32),
            pltpu.SMEM((BR,), i32),
            pltpu.SemaphoreType.DMA((2, NQ, 10)),
            pltpu.SemaphoreType.DMA((2, NQ, 10)),
            pltpu.SemaphoreType.DMA((MP - 1,)),
            pltpu.SemaphoreType.DMA((MP - 1,)),
            pltpu.SemaphoreType.DMA,
            pltpu.SemaphoreType.DMA((MP, 3)),
            pltpu.SemaphoreType.DMA((6,)),
            pltpu.SemaphoreType.DMA,
        ],
        compiler_params=pltpu.CompilerParams(
            collective_id=0, has_side_effects=True, vmem_limit_bytes=44 * 2**20),
        name="relay_pages_and_attend",
    )(*operands)
    refilled, attention = pl.pallas_call(
        refill_kernel,
        out_shape=(
            jax.ShapeDtypeStruct(pool.shape, bf16),
            jax.ShapeDtypeStruct((BR, HEADS * HD), bf16),
        ),
        in_specs=[vmem] * 5 + [smem],
        out_specs=(hbm, vmem),
        scratch_shapes=[
            pltpu.VMEM(pool.shape, bf16),
            *chunk,
            pltpu.VMEM((SLOTS * HEADS, HD), f32),
            pltpu.VMEM((BR, HEADS, HD), f32),
            pltpu.SemaphoreType.DMA((RANGES,)),
        ],
        compiler_params=pltpu.CompilerParams(vmem_limit_bytes=44 * 2**20),
        name="refill_pool",
    )(*kept, places)
    return (refilled.reshape(kv_pool.shape), attention)


def solution(mesh):
    return jax.shard_map(
        shards,
        mesh=mesh,
        in_specs=(
            P("dp", "mp"),
            P(None, "mp"),
            P(None, "mp"),
            P(None, "mp"),
            P(),
            P(),
            P("dp", None, "mp", None),
            P(),
            P(),
            P(),
        ),
        out_specs=(P("dp", None, "mp", None), P("dp", "mp")),
        check_vma=False,
    )
```

```python
import math

import jax
import jax.numpy as jnp
from jax import lax
from jax.experimental import pallas as pl
from jax.experimental.pallas import tpu as pltpu
from jax.sharding import PartitionSpec as P

H = 64
KVH = 8
HD = 128
PAGE = 16
NPAGE = 48
BR = 16
GROUPS = 16
ALIVE = 4
KIDS = 14
SIDE = 4
NQ = 2
PQ = 3
PIECE = NQ * PQ
HALF = NPAGE // 2
MP = 8
MESH = pl.DeviceIdType.MESH
SLOTS = ALIVE + KIDS
CHUNK_TOKENS = SIDE * PQ * PAGE
HEADS = H // KVH
RANGES = 12
BATCH = 7


def attend_chunk(arrived, queries, scores, terms, mixes, peak, mass, mixed, q, first, count):
    rows = pl.ds(first * HEADS, count * HEADS)
    windows = [
        jnp.concatenate(
            [arrived[half, q, :, first + j].reshape(CHUNK_TOKENS, 2 * HD) for half in range(2)], axis=0)
        for j in range(count)
    ]
    for j in range(count):
        query = queries[pl.ds((first + j) * HEADS, HEADS)].astype(jnp.bfloat16)
        scores[pl.ds(j * HEADS, HEADS)] = lax.dot_general(
            query, windows[j][:, :HD], (((1,), (1,)), ((), ())), preferred_element_type=jnp.float32)
    part = pl.ds(0, count * HEADS)
    all_scores = scores[part]
    old = peak[rows]
    new = jnp.maximum(old, jnp.max(all_scores, -1, keepdims=True))
    scale = jnp.exp(old - new)
    all_terms = jnp.exp(all_scores - new[:, :1])
    terms[part] = all_terms
    for j in range(count):
        weights = terms[pl.ds(j * HEADS, HEADS)].astype(jnp.bfloat16)
        mixes[pl.ds(j * HEADS, HEADS)] = jnp.dot(
            weights, windows[j][:, HD:], preferred_element_type=jnp.float32)
    new_mass = mass[rows] * scale + jnp.sum(all_terms, -1, keepdims=True)
    return new, new_mass, mixed[rows] * scale + mixes[part]


def relay_kernel(
    hidden_ref, query_gain_hbm, key_gain_hbm, w_query_ref, w_key_ref, w_value_ref, pool_ref,
    table_hbm, parent_hbm, surviving_hbm,
    arrived, slot_queries, peak, mass, mixed, places_ref,
    *scratch,
):
    scratch = list(scratch)
    gathered = [scratch.pop(0) for _ in range(NQ)]
    (outgoing, pool, features, w_query, w_key, w_value, project, queries, keys, values,
     scores, terms, mixes, places,
     query_gain_ref, key_gain_ref, table_ref, parent_ref, surviving_ref,
     alive_table, rank_table, source_table, child_table, slot_table,
     send_sem, recv_sem, feature_send, feature_recv, pool_sem, weight_sem, small_sem, places_sem) = scratch

    group = lax.axis_index("dp")
    part = lax.axis_index("mp")
    z, y = group // SIDE, group % SIDE

    def device(half, gather_at, spread_at):
        if half == 0:
            return (gather_at * SIDE + spread_at, part)
        return (spread_at * SIDE + gather_at, part)

    def shifted(value, step, size=SIDE):
        return (value + step + size) % size

    pool_copy = pltpu.make_async_copy(pool_ref, pool, pool_sem)
    barrier = pltpu.get_barrier_semaphore()
    def greet_line(step, carry):
        pl.semaphore_signal(barrier, inc=1, device_id=device(0, z, shifted(y, step)), device_id_type=MESH)
        pl.semaphore_signal(barrier, inc=1, device_id=device(1, y, shifted(z, step)), device_id_type=MESH)
        return carry

    def greet_part(step, carry):
        pl.semaphore_signal(barrier, inc=1, device_id=(group, shifted(part, step, MP)), device_id_type=MESH)
        return carry

    lax.fori_loop(1, SIDE, greet_line, 0)
    lax.fori_loop(1, MP, greet_part, 0)

    small_copies = [
        pltpu.make_async_copy(source, target, small_sem.at[i])
        for i, (source, target) in enumerate((
            (surviving_hbm, surviving_ref), (parent_hbm, parent_ref), (table_hbm, table_ref),
            (query_gain_hbm, query_gain_ref), (key_gain_hbm, key_gain_ref),
            (hidden_ref, features.at[part])))
    ]
    for copy in small_copies:
        copy.start()
    pool_copy.start()

    def rank_group(at, carry):
        found = [jnp.int32(99) for _ in range(ALIVE)]
        count = jnp.int32(0)
        for branch in range(BR):
            lives = surviving_ref[at * BR + branch]
            rank_table[at * BR + branch] = count
            for k in range(ALIVE):
                found[k] = jnp.where((lives > 0) & (count == k), jnp.int32(branch), found[k])
            count = count + lives
        for k in range(ALIVE):
            alive_table[at * ALIVE + k] = found[k]
        return carry

    def child_of(at_group, j):
        branch = j
        for k in range(ALIVE):
            branch = branch + jnp.where(alive_table[at_group * ALIVE + k] - k <= j, 1, 0)
        return jnp.minimum(branch, BR - 1)

    def find_sources():
        for half in range(2):
            for spread_at in range(SIDE):
                target = z * SIDE + spread_at if half == 0 else spread_at * SIDE + y

                def find_source(j, carry, half=half, spread_at=spread_at, target=target):
                    parent = parent_ref[target * BR + child_of(target, j)]
                    from_group = parent // BR
                    rank = rank_table[parent]
                    if half == 1:
                        from_group = (from_group % SIDE) * SIDE + from_group // SIDE
                    source_table[(half * SIDE + spread_at) * KIDS + j] = (half * GROUPS + from_group) * ALIVE + rank
                    return carry

                lax.fori_loop(0, KIDS, find_source, 0)

        def own_children(j, carry):
            child_table[j] = child_of(group, j)
            return carry

        lax.fori_loop(0, KIDS, own_children, 0)

        def own_slots(b, carry):
            rank = rank_table[group * BR + b]
            lives = surviving_ref[group * BR + b]
            slot_table[b] = jnp.minimum(jnp.where(lives > 0, rank, ALIVE + b - rank), SLOTS - 1)
            return carry

        lax.fori_loop(0, BR, own_slots, 0)

    def invert_table():
        row = lax.broadcasted_iota(jnp.int32, (8, 128), 0)
        lane = lax.broadcasted_iota(jnp.int32, (8, 128), 1)
        page_ids = row * 128 + lane

        def one_branch(b, found):
            slot = slot_table[b]
            found = jnp.where((row == 7) & (lane == b), slot, found)
            for half in range(2):
                for c in range(SIDE):
                    for q in range(NQ):
                        for r in range(PQ):
                            page = table_ref[half * HALF + c * PIECE + q * PQ + r, group * BR + b]
                            place = (((half * NQ + q) * SIDE + c) * SLOTS + slot) * PQ + r
                            found = jnp.where(page_ids == page, place, found)
            return found

        places[...] = lax.fori_loop(0, BR, one_branch, jnp.zeros((8, 128), jnp.int32))
        copy = pltpu.make_async_copy(places, places_ref, places_sem)
        copy.start()
        copy.wait()

    feature_copies, weight_copies = [], []
    rows = hidden_ref.shape[1]

    def send_features():
        for step in range(1, MP):
            copy = pltpu.make_async_remote_copy(
                src_ref=hidden_ref, dst_ref=features.at[part],
                send_sem=feature_send.at[step - 1], recv_sem=feature_recv.at[step - 1],
                device_id=(group, shifted(part, step, MP)), device_id_type=MESH)
            copy.start()
            feature_copies.append(copy)

    def load_weights():
        for m in range(MP):
            some = pl.ds(m * rows, rows)
            copies = [
                pltpu.make_async_copy(source.at[some], target.at[some], weight_sem.at[m, i])
                for i, (source, target) in enumerate(
                    ((w_query_ref, w_query), (w_key_ref, w_key), (w_value_ref, w_value)))
            ]
            for copy in copies:
                copy.start()
            weight_copies.append(copies)

    def remote(half, q, kind, source, target, gather_at, spread_at):
        to = jnp.where(half == 0, gather_at * SIDE + spread_at, spread_at * SIDE + gather_at)
        return pltpu.make_async_remote_copy(
            src_ref=source, dst_ref=target,
            send_sem=send_sem.at[half, q, kind], recv_sem=recv_sem.at[half, q, kind],
            device_id=(to, part), device_id_type=MESH)

    def place_of(half):
        return jnp.where(half == 0, z, y), jnp.where(half == 0, y, z)

    def each_half(body):
        def run(half, carry):
            body(half, *place_of(half))
            return carry

        lax.fori_loop(0, 2, run, 0)

    def each_step(first, last, body):
        def run(step, carry):
            body(step)
            return carry

        lax.fori_loop(first, last, run, 0)

    def pack_alive(q):
        def one(k, carry):
            branch = group * BR + jnp.minimum(alive_table[group * ALIVE + k], BR - 1)
            for half in range(2):
                where = [(spread_at, r) for spread_at in range(SIDE) for r in range(PQ)]
                pages = [table_ref[half * HALF + spread_at * PIECE + q * PQ + r, branch] for spread_at, r in where]
                blocks = [pool[page] for page in pages]
                for (spread_at, r), block in zip(where, blocks):
                    arrived[half, q, spread_at, k, r] = block
            return carry

        lax.fori_loop(0, ALIVE, one, 0)

    def spread_copy(q, half, a, c, step):
        to = shifted(c, step)
        here = pl.ds(half * 64 + a * 16 + c * 4, 4)
        return remote(
            half, q, step - 1, arrived.at[half, q, to, pl.ds(0, ALIVE)], gathered[q].at[here], a, to)

    def spread(q):
        def one(half, a, c):
            each_step(1, SIDE, lambda step: spread_copy(q, half, a, c, step).start())
            gathered[q][pl.ds(half * 64 + a * 16 + c * 4, 4)] = arrived[half, q, c, 0:ALIVE]

        each_half(one)

    def gather_copy(q, half, a, c, way):
        block = gathered[q].at[pl.ds(half * 64 + a * 16, 16)]
        return remote(half, q, 3 + way, block, block, shifted(a, 1 - 2 * way), c)

    def gather(q):
        def one(half, a, c):
            each_step(1, SIDE, lambda step: spread_copy(q, half, a, c, step).wait_recv())
            each_step(0, 2, lambda way: gather_copy(q, half, a, c, way).start())

        each_half(one)

    def forward_copy(q, half, a, c, way):
        step = 1 - 2 * way
        block = gathered[q].at[pl.ds(half * 64 + shifted(a, -step) * 16 + way * 8, 8)]
        return remote(half, q, 5 + way, block, block, shifted(a, step), c)

    def forward(q):
        def one(half, a, c):
            each_step(0, 2, lambda way: gather_copy(q, half, a, c, way).wait_recv())
            each_step(0, 2, lambda way: forward_copy(q, half, a, c, way).start())

        each_half(one)

    def deliver_copy(q, half, a, c, step):
        return remote(
            half, q, 6 + step, outgoing.at[half, q, step - 1],
            arrived.at[half, q, c, pl.ds(ALIVE, KIDS)], a, shifted(c, step))

    def deliver(q):
        each_half(lambda half, a, c: each_step(
            0, 2, lambda way: forward_copy(q, half, a, c, way).wait_recv()))

        def one(half, a, c):
            def pack(to, put):
                def few(batch, carry):
                    slots = [batch * BATCH + i for i in range(BATCH)]
                    sources = [source_table[(half * SIDE + to) * KIDS + j] for j in slots]
                    blocks = [gathered[q][source] for source in sources]
                    for j, block in zip(slots, blocks):
                        put(j, block)
                    return carry

                lax.fori_loop(0, KIDS // BATCH, few, 0)

            def send(step):
                def put(j, block):
                    outgoing[half, q, step - 1, j] = block

                pack(shifted(c, step), put)
                deliver_copy(q, half, a, c, step).start()

            def keep(j, block):
                arrived[half, q, c, ALIVE + j] = block

            each_step(1, SIDE, send)
            pack(c, keep)

        each_half(one)

    def wait_delivered(q):
        each_half(lambda half, a, c: each_step(
            1, SIDE, lambda step: deliver_copy(q, half, a, c, step).wait_recv()))

    def wait_sent(q):
        def one(half, a, c):
            each_step(1, SIDE, lambda step: spread_copy(q, half, a, c, step).wait_send())
            each_step(0, 2, lambda way: gather_copy(q, half, a, c, way).wait_send())
            each_step(0, 2, lambda way: forward_copy(q, half, a, c, way).wait_send())

        each_half(one)

    def wait_delivery_sent(q):
        each_half(lambda half, a, c: each_step(
            1, SIDE, lambda step: deliver_copy(q, half, a, c, step).wait_send()))

    def normalize(block, gain):
        return block * lax.rsqrt(jnp.mean(block * block, -1, keepdims=True) + 1e-06) * gain

    def project_tokens():
        for copy in small_copies[3:]:
            copy.wait()
        for copy in feature_copies:
            copy.wait_recv()
        project[...] = jnp.zeros_like(project)
        for m in range(MP):
            for copy in weight_copies[m]:
                copy.wait()
            some = pl.ds(m * rows, rows)
            part_rows = features[m]
            for i in range(4):
                columns = pl.ds(i * 256, 256)
                project[:, columns] += jnp.dot(
                    part_rows, w_query[some, columns], preferred_element_type=jnp.float32)
            project[:, pl.ds(1024, HD)] += jnp.dot(part_rows, w_key[some], preferred_element_type=jnp.float32)
            project[:, pl.ds(1152, HD)] += jnp.dot(part_rows, w_value[some], preferred_element_type=jnp.float32)
        for head in range(HEADS):
            block = normalize(project[:, pl.ds(head * HD, HD)], query_gain_ref[...]) / math.sqrt(HD)
            queries[:, head, :] = block.astype(jnp.bfloat16).astype(jnp.float32)
        key_rows = normalize(project[:, pl.ds(1024, HD)], key_gain_ref[...])
        keys[:, 0, :] = key_rows.astype(jnp.bfloat16).astype(jnp.float32)
        values[:, 0, :] = project[:, pl.ds(1152, HD)].astype(jnp.bfloat16).astype(jnp.float32)

    def start_attention():
        for slot in range(SLOTS):
            if slot < ALIVE:
                branch = jnp.minimum(alive_table[group * ALIVE + slot], BR - 1)
            else:
                branch = child_table[slot - ALIVE]
            some = pl.ds(slot * HEADS, HEADS)
            query = queries[branch]
            slot_queries[some] = query
            own_score = jnp.sum(query * keys[branch], -1, keepdims=True)
            peak[some] = jnp.broadcast_to(own_score, (HEADS, HD))
            mass[some] = jnp.ones((HEADS, HD), jnp.float32)
            mixed[some] = jnp.broadcast_to(values[branch], (HEADS, HD))

    def attend(q, first, count):
        some = pl.ds(first * HEADS, count * HEADS)
        peak[some], mass[some], mixed[some] = attend_chunk(
            arrived, slot_queries, scores, terms, mixes, peak, mass, mixed, q, first, count)

    small_copies[0].wait()
    rank_group(group, 0)
    small_copies[2].wait()
    pool_copy.wait()
    pack_alive(0)
    pl.semaphore_wait(barrier, 2 * (SIDE - 1) + MP - 1)
    spread(0)
    for q in range(1, NQ):
        pack_alive(q)
        spread(q)
    send_features()
    load_weights()
    small_copies[1].wait()
    lax.fori_loop(0, GROUPS, rank_group, 0)
    find_sources()
    for q in range(NQ):
        gather(q)
    for q in range(NQ):
        forward(q)
    for q in range(NQ):
        deliver(q)
    invert_table()
    project_tokens()
    start_attention()
    for q in range(NQ):
        attend(q, 0, ALIVE)
    done = pl.ds(0, ALIVE * HEADS)
    mixed[done] = mixed[done] / mass[done]
    for q in range(NQ - 1):
        wait_delivered(q)
        attend(q, ALIVE, KIDS)
    for q in range(NQ):
        wait_sent(q)
        if q < NQ - 1:
            wait_delivery_sent(q)
    for copy in feature_copies:
        copy.wait_send()
    wait_delivered(NQ - 1)
    wait_delivery_sent(NQ - 1)


def refill_kernel(
    arrived, slot_queries, peak, mass, mixed, places_ref,
    refilled_ref, attention_ref,
    refilled, scores, terms, mixes, final, result, store_sem,
):
    pages = arrived.reshape(2 * NQ * SIDE * SLOTS * PQ, PAGE, 2 * HD)
    stores = [
        pltpu.make_async_copy(
            refilled.at[pl.ds(part * 64, 64)], refilled_ref.at[pl.ds(part * 64, 64)], store_sem.at[part])
        for part in range(RANGES)
    ]

    def place(part, carry):
        for batch in range(4):
            at = [batch * 16 + i for i in range(16)]
            places = [places_ref[part // 2, part % 2 * 64 + i] for i in at]
            blocks = [pages[place] for place in places]
            for i, block in zip(at, blocks):
                refilled[part * 64 + i] = block
        some = pl.ds(part * 64, 64)
        pltpu.make_async_copy(refilled.at[some], refilled_ref.at[some], store_sem.at[part]).start()
        return carry

    lax.fori_loop(0, RANGES, place, 0)
    alive = pl.ds(0, ALIVE * HEADS)
    final[alive] = mixed[alive]
    _, total, mix = attend_chunk(
        arrived, slot_queries, scores, terms, mixes, peak, mass, mixed, NQ - 1, ALIVE, KIDS)
    final[pl.ds(ALIVE * HEADS, KIDS * HEADS)] = mix / total
    for b in range(BR):
        result[b] = final[pl.ds(pl.multiple_of(places_ref[7, b] * HEADS, HEADS), HEADS)]
    for head in range(HEADS):
        attention_ref[:, pl.ds(head * HD, HD)] = result[:, head, :].astype(jnp.bfloat16)
    for copy in stores:
        copy.wait()


def shards(
    hidden, w_query, w_key, w_value, query_gain, key_gain, kv_pool, page_table, parent, surviving
):
    pool_pages = kv_pool.shape[0]
    pool = kv_pool.reshape(pool_pages, PAGE, 2 * HD)
    table = page_table.T
    vmem = pl.BlockSpec(memory_space=pltpu.VMEM)
    smem = pl.BlockSpec(memory_space=pltpu.SMEM)
    hbm = pl.BlockSpec(memory_space=pltpu.HBM)
    bf16, f32, i32 = jnp.bfloat16, jnp.float32, jnp.int32
    page_shape = (PAGE, 2 * HD)
    state = pltpu.VMEM((SLOTS * HEADS, HD), f32)
    chunk = [
        pltpu.VMEM((KIDS * HEADS, 2 * CHUNK_TOKENS), f32),
        pltpu.VMEM((KIDS * HEADS, 2 * CHUNK_TOKENS), f32),
        pltpu.VMEM((KIDS * HEADS, HD), f32),
    ]
    operands = [
        pltpu.with_memory_space_constraint(x, pltpu.HBM)
        for x in (hidden, query_gain.reshape(1, HD), key_gain.reshape(1, HD), w_query, w_key, w_value, pool,
                  table, parent, surviving)
    ]
    *kept, places = pl.pallas_call(
        relay_kernel,
        out_shape=(
            pltpu.VMEM((2, NQ, SIDE, SLOTS, PQ) + page_shape, bf16),
            state, state, state, state,
            pltpu.SMEM((8, 128), i32),
        ),
        in_specs=[hbm] * 10,
        out_specs=(vmem,) * 5 + (smem,),
        scratch_shapes=[pltpu.VMEM((2 * GROUPS * ALIVE, PQ) + page_shape, bf16)] * NQ
        + [
            pltpu.VMEM((2, NQ, SIDE - 1, KIDS, PQ) + page_shape, bf16),
            pltpu.VMEM(pool.shape, bf16),
            pltpu.VMEM((MP,) + hidden.shape, bf16),
            pltpu.VMEM(w_query.shape, bf16),
            pltpu.VMEM(w_key.shape, bf16),
            pltpu.VMEM(w_value.shape, bf16),
            pltpu.VMEM((BR, HEADS * HD + 2 * HD), f32),
            pltpu.VMEM((BR, HEADS, HD), f32),
            pltpu.VMEM((BR, 1, HD), f32),
            pltpu.VMEM((BR, 1, HD), f32),
            *chunk,
            pltpu.VMEM((8, 128), i32),
            pltpu.VMEM((1, HD), f32),
            pltpu.VMEM((1, HD), f32),
            pltpu.SMEM(table.shape, i32),
            pltpu.SMEM(parent.shape, i32),
            pltpu.SMEM(surviving.shape, i32),
            pltpu.SMEM((GROUPS * ALIVE,), i32),
            pltpu.SMEM((GROUPS * BR,), i32),
            pltpu.SMEM((2 * SIDE * KIDS,), i32),
            pltpu.SMEM((KIDS,), i32),
            pltpu.SMEM((BR,), i32),
            pltpu.SemaphoreType.DMA((2, NQ, 10)),
            pltpu.SemaphoreType.DMA((2, NQ, 10)),
            pltpu.SemaphoreType.DMA((MP - 1,)),
            pltpu.SemaphoreType.DMA((MP - 1,)),
            pltpu.SemaphoreType.DMA,
            pltpu.SemaphoreType.DMA((MP, 3)),
            pltpu.SemaphoreType.DMA((6,)),
            pltpu.SemaphoreType.DMA,
        ],
        compiler_params=pltpu.CompilerParams(
            collective_id=0, has_side_effects=True, vmem_limit_bytes=44 * 2**20),
        name="relay_pages_and_attend",
    )(*operands)
    refilled, attention = pl.pallas_call(
        refill_kernel,
        out_shape=(
            jax.ShapeDtypeStruct(pool.shape, bf16),
            jax.ShapeDtypeStruct((BR, HEADS * HD), bf16),
        ),
        in_specs=[vmem] * 5 + [smem],
        out_specs=(hbm, vmem),
        scratch_shapes=[
            pltpu.VMEM(pool.shape, bf16),
            *chunk,
            pltpu.VMEM((SLOTS * HEADS, HD), f32),
            pltpu.VMEM((BR, HEADS, HD), f32),
            pltpu.SemaphoreType.DMA((RANGES,)),
        ],
        compiler_params=pltpu.CompilerParams(vmem_limit_bytes=44 * 2**20),
        name="refill_pool",
    )(*kept, places)
    return (refilled.reshape(kv_pool.shape), attention)


def solution(mesh):
    return jax.shard_map(
        shards,
        mesh=mesh,
        in_specs=(
            P("dp", "mp"),
            P(None, "mp"),
            P(None, "mp"),
            P(None, "mp"),
            P(),
            P(),
            P("dp", None, "mp", None),
            P(),
            P(),
            P(),
        ),
        out_specs=(P("dp", None, "mp", None), P("dp", "mp")),
        check_vma=False,
    )
```
